32 devices in a mesh: enc: 4 (over z), kr: 2 (over y), kc: 4 (over x, core).
Axes of the slice: x: 2, y: 2, z: 4, core: 2. Of those that a mesh axis runs over, the one named last changes fastest.
Arguments:
- inputs: bfloat16 [6144, 1024], P(('enc', 'kr', 'kc')), may hold values from -6 to 6
- w_first: bfloat16 [1024, 1024], replicated, may hold values from -0.1875 to 0.1875
- w_second: bfloat16 [1024, 64], replicated, may hold values from -0.1875 to 0.1875
- inv_length: float32 [64], replicated, may hold values from 0.05 to 1.8
- probes: bfloat16 [6144, 128], P(('enc', 'kr', 'kc')), may hold values from -6 to 6
- solves: bfloat16 [6144, 128], P(('enc', 'kr', 'kc')), may hold values from -6 to 6
Outputs:
- products: bfloat16 [6144, 128], P(('enc', 'kr', 'kc'))
- grad_first: float32 [1024, 1024], P(('enc', 'kr', 'kc'))
- grad_second: float32 [1024, 64], P(('enc', 'kr', 'kc'))
The draws below stay inside these ranges and needn't reach their ends.
All inputs are finite; a program needn't handle non-finite values.
Results may differ from the reference program's by a relative error of at most 0.007.
The reference program's roundings to bfloat16 on the way count: a program that leaves them out, or rounds other values in their place, can miss the bound.
Values may be sent and summed in bfloat16 or wider, within the bound.
No kernel may reach another device: no remote copies, remote signals or barrier semaphores. Data moves between devices by JAX's collectives and lax.ppermute only.
A program may use at most 64 MiB of HBM per device.

```python
import math
import jax
import jax.numpy as jnp
from jax import lax

IN = 1024
HID = 1024
FEAT = 64
PROBES = 128
ROWS = 6144


def draw_inv_length(key, part):
    base_key = jax.random.fold_in(key, 7)
    pick_key, narrow_key, broad_key = jax.random.split(base_key, 3)
    ranking = jax.random.permutation(pick_key, FEAT)
    narrow_mask = ranking < FEAT // 4
    narrow_scale = jnp.exp(jax.random.uniform(narrow_key, (FEAT,), jnp.float32, math.log(0.9), math.log(1.8)))
    broad_scale = jnp.exp(jax.random.uniform(broad_key, (FEAT,), jnp.float32, math.log(0.05), math.log(0.3)))
    return jnp.where(narrow_mask, narrow_scale, broad_scale).astype(jnp.float32)


def strengthened(array, key, source, target, parts, factor):
    owner, partner = [(jnp.arange(array.shape[dim]) // (array.shape[dim] // parts)).reshape([-1 if axis == dim else 1 for axis in range(array.ndim)]) for dim in (source, target)]
    chosen = jax.random.permutation(key, parts)[partner]
    strong = (owner == chosen) | (owner == (partner + parts // 2) % parts)
    return jnp.where(strong, factor * array, array)


def level_of(stream_key, dims, cuts, low, top_value):
    def one(axis_at, parts):
        draws = jax.random.uniform(jax.random.fold_in(jax.random.fold_in(stream_key, 6), axis_at), (parts,), jnp.float32, low / len(cuts), top_value / len(cuts))
        return jnp.repeat(jnp.exp(draws), dims[axis_at] // parts).reshape((-1,) + (1,) * (len(dims) - axis_at - 1))

    loudness = one(*cuts[0])
    for cut in cuts[1:]:
        loudness = loudness * one(*cut)
    return loudness


def normal_values(rng, shape, scale, most, pieces=(), kind=jnp.bfloat16):
    drawn = jax.random.normal(rng, shape, jnp.float32) * scale
    if len(pieces) > 0:
        drawn = level_of(rng, shape, pieces, -0.22, 0.18) * drawn
    return jnp.clip(drawn, min=-most, max=most).astype(kind)


def bell_draw_with(own_key, dims, deviation, most, pieces, heavy, kind=jnp.bfloat16):
    drawn = deviation * jax.random.normal(own_key, dims, jnp.float32)
    if pieces:
        drawn = drawn * level_of(own_key, dims, pieces, -0.22, 0.18)
    return jnp.clip(strengthened(drawn, jax.random.fold_in(own_key, 3), *heavy), -most, most).astype(kind)


def setup_inputs(seed: int = 0) -> dict:
    key_list = jax.random.split(jax.random.key(seed), 7)
    inputs = bell_draw_with(key_list[0], (ROWS, IN), 1.0, 6.0, ((0, 32),), (0, 1, 32, 2.75))
    w_first = normal_values(key_list[1], (IN, HID), IN ** -0.5, 0.1875)
    w_second = normal_values(key_list[2], (HID, FEAT), HID ** -0.5, 0.1875)
    inv_length = draw_inv_length(jax.random.fold_in(key_list[6], 71), 0)
    probes = normal_values(key_list[4], (ROWS, PROBES), 1.0, 6.0, ((0, 32),))
    solves = normal_values(key_list[5], (ROWS, PROBES), 1.0, 6.0, ((0, 32),))
    return {"inputs": inputs, "w_first": w_first, "w_second": w_second, "inv_length": inv_length, "probes": probes, "solves": solves}


probe_gain = 0.5
loss_gain = 0.02

def contract_inner(left, right):
    return lax.dot_general(left, right, (((1,), (1,)), ((), ())), preferred_element_type=jnp.float32)

def contract_outer(left, right):
    return lax.dot_general(left, right, (((0,), (0,)), ((), ())), preferred_element_type=jnp.float32)

def reference(inputs, w_first, w_second, inv_length, probes, solves):
    pre = jnp.dot(inputs, w_first, preferred_element_type=jnp.float32)
    hidden = jax.nn.silu(pre).astype(jnp.bfloat16)
    features = jnp.dot(hidden, w_second, preferred_element_type=jnp.float32)
    scaled = (features * inv_length[None, :]).astype(jnp.bfloat16)
    widened = scaled.astype(jnp.float32)
    norms = lax.optimization_barrier(jnp.sum(widened * widened, axis=1))
    total = scaled.shape[0]
    block_rows = min(512, total)
    count = total // block_rows

    def per_block(index):
        offset = (index * block_rows).astype(jnp.int32)
        row_feat = lax.dynamic_slice_in_dim(scaled, offset, block_rows, 0)
        row_norm = lax.dynamic_slice_in_dim(norms, offset, block_rows, 0)
        row_probe = lax.dynamic_slice_in_dim(probes, offset, block_rows, 0)
        row_solve = lax.dynamic_slice_in_dim(solves, offset, block_rows, 0)
        cross = contract_inner(row_feat, scaled)
        kernel = jnp.exp(-0.5 * (row_norm[:, None] + norms[None, :] - 2.0 * cross))
        vsum = jnp.dot(kernel.astype(jnp.bfloat16), probes, preferred_element_type=jnp.float32)
        first = kernel * contract_inner(row_solve, probes)
        second = kernel * contract_inner(row_probe, solves)
        sums = lax.optimization_barrier(jnp.sum(first, axis=1)) + lax.optimization_barrier(jnp.sum(second, axis=1))
        mixed = jnp.dot(first.astype(jnp.bfloat16), scaled, preferred_element_type=jnp.float32) + jnp.dot(second.astype(jnp.bfloat16), scaled, preferred_element_type=jnp.float32)
        return (vsum, mixed, sums)
    vsum, mixed, sums = lax.map(per_block, jnp.arange(count, dtype=jnp.int32))
    vsum = vsum.reshape(total, probes.shape[1])
    mixed = mixed.reshape(total, scaled.shape[1])
    sums = sums.reshape(total)
    products = (vsum * probe_gain).astype(jnp.bfloat16)
    lscale = loss_gain / math.sqrt(probes.shape[1])
    dfeat = -lscale * inv_length[None, :] * (sums[:, None] * widened - mixed)
    dfeat_half = dfeat.astype(jnp.bfloat16)
    grad_second = contract_outer(hidden, dfeat_half)
    back_hidden = contract_inner(dfeat_half, w_second)
    sigma = jax.nn.sigmoid(pre)
    dpre = (back_hidden * sigma * (1.0 + pre * (1.0 - sigma))).astype(jnp.bfloat16)
    grad_first = contract_outer(inputs, dpre)
    return (products, grad_first, grad_second)
```

```python
import math

import jax
import jax.numpy as jnp
from jax import lax
from jax.experimental import pallas as pl
from jax.experimental.pallas import tpu as pltpu
from jax.sharding import PartitionSpec as P

probe_gain = 0.5
loss_gain = 0.02
F32 = jnp.float32
BF16 = jnp.bfloat16
VMEM_LIMIT = 48 * 1024 * 1024


def dot_nn(left, right):
    return lax.dot_general(left, right, (((1,), (0,)), ((), ())), preferred_element_type=F32)


def dot_nt(left, right):
    return lax.dot_general(left, right, (((1,), (1,)), ((), ())), preferred_element_type=F32)


def swap(x, axis, mask):
    size = lax.axis_size(axis)
    return lax.ppermute(x, axis, [(i, i ^ mask) for i in range(size)])


def gather_direct(x, axis):
    return jnp.concatenate([x] + [swap(x, axis, m) for m in range(1, lax.axis_size(axis))], axis=0)


def gather_double(x, axis):
    mask = lax.axis_size(axis) // 2
    while mask:
        x = jnp.concatenate([x, swap(x, axis, mask)], axis=0)
        mask //= 2
    return x


def pack(x):
    half = x.shape[0] // 2
    return jnp.concatenate([x[:half], x[half:]], axis=1)


def unpack_blocks(packed, rows):
    width = packed.shape[1] // 2
    p = packed.reshape(packed.shape[0] // rows, rows, packed.shape[1])
    u = jnp.concatenate([p[:, :, :width], p[:, :, width:]], axis=1)
    return u.reshape(packed.shape[0] * 2, width)


def whole_specs(n):
    return [pl.BlockSpec(memory_space=pltpu.VMEM)] * n


def encode_body(x_ref, w1_ref, w2_ref, inv_ref, out_ref, acc_ref):
    step = pl.program_id(0)
    pre = dot_nn(x_ref[...], w1_ref[...])
    hidden = (pre * jax.nn.sigmoid(pre)).astype(BF16)
    part = dot_nn(hidden, w2_ref[...])

    @pl.when(step == 0)
    def _():
        acc_ref[...] = part

    @pl.when(step > 0)
    def _():
        acc_ref[...] += part

    @pl.when(step == pl.num_programs(0) - 1)
    def _():
        out_ref[...] = pack((acc_ref[...] * inv_ref[...]).astype(BF16))


def encode(inputs, w_first, w_second, inv_row):
    rows, width = inputs.shape
    hid, feat = w_second.shape
    block = 256
    return pl.pallas_call(
        encode_body,
        grid=(hid // block,),
        in_specs=[
            pl.BlockSpec((rows, width), lambda j: (0, 0)),
            pl.BlockSpec((width, block), lambda j: (0, j)),
            pl.BlockSpec((block, feat), lambda j: (j, 0)),
            pl.BlockSpec((1, feat), lambda j: (0, 0)),
        ],
        out_specs=pl.BlockSpec((rows // 2, 2 * feat), lambda j: (0, 0)),
        out_shape=jax.ShapeDtypeStruct((rows // 2, 2 * feat), BF16),
        scratch_shapes=[pltpu.VMEM((rows, feat), F32)],
        compiler_params=pltpu.CompilerParams(vmem_limit_bytes=VMEM_LIMIT),
        name="encode",
    )(inputs, w_first, w_second, inv_row)


def pair_body(own_rows, rowf_ref, rowp_ref, colf_ref, colp_ref, v_ref, keep_ref, send_ref, rowa, cola, colu, m_acc, s_acc):
    half = own_rows // 2
    probe = v_ref.shape[1]
    ru = unpack_blocks(rowf_ref[...], half)
    rows, feat = ru.shape
    ru32 = ru.astype(F32)
    h = -0.5 * jnp.sum(ru32 * ru32, axis=1, keepdims=True)
    h1 = h.astype(BF16).astype(F32)
    h2 = (h - h1).astype(BF16).astype(F32)
    h3 = h - h1 - h2
    lane = lax.broadcasted_iota(jnp.int32, (rows, feat), 1)
    tail = jnp.where(lane == 0, h1, jnp.where(lane == 1, h2, jnp.where(lane == 2, h3, 0.0)))
    minus = jnp.full((rows, 2 * feat), -0.5, BF16)
    rowa[...] = jnp.concatenate([ru, minus, tail.astype(BF16)], axis=1)

    cu = unpack_blocks(colf_ref[...], half)
    cols = cu.shape[0]
    cu32 = cu.astype(F32)
    sq = cu32 * cu32
    hi = sq.astype(BF16)
    lo = (sq - hi.astype(F32)).astype(BF16)
    clane = lax.broadcasted_iota(jnp.int32, (cols, feat), 1)
    ones = jnp.where(clane < 3, 1.0, 0.0).astype(BF16)
    cola[...] = jnp.concatenate([cu, hi, lo, ones], axis=1)
    colu[...] = cu

    rp = rowp_ref[...]
    rsp = jnp.concatenate([rp[:, probe:], rp[:, :probe]], axis=1)
    v_ref[...] = jnp.zeros(v_ref.shape, F32)
    m_acc[...] = jnp.zeros(m_acc.shape, F32)
    s_acc[...] = jnp.zeros(s_acc.shape, F32)
    tile = 256

    def step(j, carry):
        at = pl.ds(pl.multiple_of(j * tile, tile), tile)
        kern = jnp.exp(dot_nt(rowa[...], cola[at, :]))
        ps = colp_ref[at, :]
        both = kern * dot_nt(rsp, ps)
        s_acc[...] += both[:, : tile // 2] + both[:, tile // 2 :]
        v_ref[...] += dot_nn(kern.astype(BF16), ps[:, :probe])
        m_acc[...] += dot_nn(both.astype(BF16), colu[at, :])
        return carry

    lax.fori_loop(0, cols // tile, step, 0)
    t = jnp.sum(s_acc[...], axis=1, keepdims=True) * ru32 - m_acc[...]
    q = rows // 4
    keep_ref[...] = jnp.concatenate([t[:q], t[q : 2 * q]], axis=1)
    send_ref[...] = jnp.concatenate([t[2 * q : 3 * q], t[3 * q :]], axis=1)


def pairs(own_rows, row_feat, row_probe, col_feat, col_probe):
    rows, cols = row_probe.shape[0], col_probe.shape[0]
    width = row_feat.shape[1]
    probe = row_probe.shape[1] // 2
    feat = width // 2
    out = jax.ShapeDtypeStruct((rows // 4, width), F32)
    return pl.pallas_call(
        lambda *refs: pair_body(own_rows, *refs),
        in_specs=whole_specs(4),
        out_specs=tuple(whole_specs(3)),
        out_shape=(jax.ShapeDtypeStruct((rows, probe), F32), out, out),
        scratch_shapes=[
            pltpu.VMEM((rows, 4 * feat), BF16),
            pltpu.VMEM((cols, 4 * feat), BF16),
            pltpu.VMEM((cols, feat), BF16),
            pltpu.VMEM((rows, feat), F32),
            pltpu.VMEM((rows, 128), F32),
        ],
        compiler_params=pltpu.CompilerParams(vmem_limit_bytes=VMEM_LIMIT),
        cost_estimate=pl.CostEstimate(flops=2 * rows * cols * 640, bytes_accessed=2 * (rows + cols) * 384, transcendentals=rows * cols),
        name="pairs",
    )(row_feat, row_probe, col_feat, col_probe)


def prepare_body(x_ref, w1_ref, sel_ref, slope_ref, xt_ref, ht_ref, xacc, hacc):
    step = pl.program_id(0)
    block = w1_ref.shape[1]
    pre = dot_nn(x_ref[...], w1_ref[...])
    sig = jax.nn.sigmoid(pre)
    hidden = (pre * sig).astype(BF16)
    slope_ref[...] = sig * (1.0 + pre * (1.0 - sig))
    at = pl.ds(pl.multiple_of(step * block, block), block)
    xt = dot_nt(sel_ref[...], x_ref[:, at])
    ht = dot_nt(sel_ref[...], hidden)

    @pl.when(step == 0)
    def _():
        xacc[...] = xt
        hacc[...] = ht

    @pl.when(step > 0)
    def _():
        xacc[...] += xt
        hacc[...] += ht

    @pl.when(step == pl.num_programs(0) - 1)
    def _():
        xt_ref[...] = xacc[...].astype(BF16)
        ht_ref[...] = hacc[...].astype(BF16)


def prepare(x_group, w_first, select):
    rows, width = x_group.shape
    hid = w_first.shape[1]
    mine = select.shape[0]
    block = 256
    return pl.pallas_call(
        prepare_body,
        grid=(hid // block,),
        in_specs=[
            pl.BlockSpec((rows, width), lambda j: (0, 0)),
            pl.BlockSpec((width, block), lambda j: (0, j)),
            pl.BlockSpec((mine, block), lambda j: (0, j)),
        ],
        out_specs=(
            pl.BlockSpec((rows, block), lambda j: (0, j)),
            pl.BlockSpec((mine, rows), lambda j: (0, 0)),
            pl.BlockSpec((mine, rows), lambda j: (0, 0)),
        ),
        out_shape=(
            jax.ShapeDtypeStruct((rows, hid), F32),
            jax.ShapeDtypeStruct((mine, rows), BF16),
            jax.ShapeDtypeStruct((mine, rows), BF16),
        ),
        scratch_shapes=[pltpu.VMEM((mine, rows), F32), pltpu.VMEM((mine, rows), F32)],
        compiler_params=pltpu.CompilerParams(vmem_limit_bytes=VMEM_LIMIT),
        cost_estimate=pl.CostEstimate(flops=2 * rows * width * hid, bytes_accessed=8 * 2**20, transcendentals=rows * hid),
        name="prepare",
    )(x_group, w_first, select)


def grads_body(d_ref, e_ref, w2_ref, slope_ref, xt_ref, ht_ref, out_ref):
    feat = w2_ref.shape[1]
    d, e = d_ref[...], e_ref[...]
    dfeat = jnp.concatenate([d[:, :feat], d[:, feat:], e[:, :feat], e[:, feat:]], axis=0)
    hid = slope_ref.shape[1]
    block = 256
    for j in range(hid // block):
        at = slice(j * block, (j + 1) * block)
        dpre = (dot_nt(dfeat, w2_ref[at, :]) * slope_ref[:, at]).astype(BF16)
        out_ref[:, at] = dot_nn(xt_ref[...], dpre).astype(BF16)
    out_ref[:, hid:] = dot_nn(ht_ref[...], dfeat).astype(BF16)


def grads(d, e, w_second, slope, xt, ht):
    rows, hid = slope.shape
    feat = w_second.shape[1]
    mine = xt.shape[0]
    return pl.pallas_call(
        grads_body,
        in_specs=whole_specs(6),
        out_specs=pl.BlockSpec(memory_space=pltpu.VMEM),
        out_shape=jax.ShapeDtypeStruct((mine, hid + feat), BF16),
        compiler_params=pltpu.CompilerParams(vmem_limit_bytes=VMEM_LIMIT),
        name="grads",
    )(d, e, w_second, slope, xt, ht)


def local(inputs, w_first, w_second, inv_length, probes, solves):
    own_rows, width = inputs.shape
    hid, feat = w_second.shape
    probe_width = probes.shape[1]
    line = lax.axis_size("kc")
    lines = lax.axis_size("enc") * lax.axis_size("kr")
    share = width // (line * lines)
    mine = width // line
    inv_row = inv_length[None, :]

    both = jnp.concatenate([probes, solves], axis=1)
    col_probe = gather_direct(gather_direct(both, "enc"), "kr")
    row_probe = gather_double(both, "kc")
    x_group = gather_double(inputs, "kc")

    scaled = encode(inputs, w_first, w_second, inv_row)
    col_feat = gather_direct(gather_direct(scaled, "enc"), "kr")
    row_feat = gather_double(scaled, "kc")

    at_row = lax.broadcasted_iota(jnp.int32, (mine, width), 0)
    at_col = lax.broadcasted_iota(jnp.int32, (mine, width), 1)
    owner = share * (line * (at_row // share) + lax.axis_index("kc")) + at_row % share
    select = (at_col == owner).astype(BF16)
    slope, xt, ht = prepare(x_group, w_first, select)

    vsum, keep, send = pairs(own_rows, row_feat, row_probe, col_feat, col_probe)
    term = keep + swap(send, "kc", 1)
    far = swap(term, "kc", 2)
    term = term + jnp.concatenate([far[:, feat:], far[:, :feat]], axis=1)
    lscale = loss_gain / math.sqrt(probe_width)
    inv_two = jnp.concatenate([inv_row, inv_row], axis=1)
    dfeat = (-lscale * inv_two * term).astype(BF16)
    other = swap(dfeat, "kc", 1)
    part = grads(dfeat, other, w_second, slope, xt, ht)
    got = lax.all_to_all(part, ("enc", "kr"), 0, 0, tiled=True)
    total = jnp.sum(got.reshape(lines, share, hid + feat).astype(F32), axis=0)

    half = vsum.shape[0] // 2
    v = vsum[:half] + swap(vsum[half:], "kc", 1)
    v = v[:own_rows] + swap(v[own_rows:], "kc", 2)
    products = (v * probe_gain).astype(BF16)
    return products, total[:, :hid], total[:, hid:]


def solution(mesh):
    rows = P(("enc", "kr", "kc"), None)
    return jax.shard_map(
        local,
        mesh=mesh,
        in_specs=(rows, P(), P(), P(), rows, rows),
        out_specs=(rows, rows, rows),
        check_vma=False,
    )
```

```python
import math

import jax
import jax.numpy as jnp
from jax import lax
from jax.experimental import pallas as pl
from jax.experimental.pallas import tpu as pltpu
from jax.sharding import PartitionSpec as P

probe_gain = 0.5
loss_gain = 0.02
F32 = jnp.float32
BF16 = jnp.bfloat16
VMEM_LIMIT = 48 * 1024 * 1024
VMEM_MOST = 60 * 1024 * 1024
VMEM = pl.BlockSpec(memory_space=pltpu.VMEM)
HBM = pl.BlockSpec(memory_space=pltpu.HBM)
ANY = pl.BlockSpec(memory_space=pl.ANY)


def dot_nn(left, right):
    return lax.dot_general(left, right, (((1,), (0,)), ((), ())), preferred_element_type=F32)


def dot_nt(left, right):
    return lax.dot_general(left, right, (((1,), (1,)), ((), ())), preferred_element_type=F32)


def swap(x, axis, mask):
    size = lax.axis_size(axis)
    return lax.ppermute(x, axis, [(i, i ^ mask) for i in range(size)])


def swap_both(x, deep_mask, tall_mask):
    deep, tall = lax.axis_size("enc"), lax.axis_size("kr")
    pairs_of = [(i, ((i // tall) ^ deep_mask) * tall + ((i % tall) ^ tall_mask)) for i in range(deep * tall)]
    return lax.ppermute(x, ("enc", "kr"), pairs_of)


def params(limit=VMEM_LIMIT):
    return pltpu.CompilerParams(vmem_limit_bytes=limit)


def encode_body(x_hbm, w1_hbm, w2t_hbm, inv_hbm, probe_hbm, solve_hbm, out_ref, x_ref, w1_ref, w2t_ref, inv_ref, sems):
    rows, width = x_ref.shape
    hid = w1_ref.shape[1]
    parts = 4
    block = hid // parts
    x_copy = pltpu.make_async_copy(x_hbm, x_ref, sems.at[0])
    w2_copy = pltpu.make_async_copy(w2t_hbm, w2t_ref, sems.at[1])
    probe_copy = pltpu.make_async_copy(probe_hbm, out_ref.at[pl.ds(0, rows), :], sems.at[2])
    solve_copy = pltpu.make_async_copy(solve_hbm, out_ref.at[pl.ds(rows, rows), :], sems.at[3])
    w1_copies = [
        pltpu.make_async_copy(w1_hbm.at[:, pl.ds(j * block, block)], w1_ref.at[:, pl.ds(j * block, block)], sems.at[4 + j])
        for j in range(parts)
    ]
    x_copy.start()
    w1_copies[0].start()
    w2_copy.start()
    for copy in w1_copies[1:]:
        copy.start()
    inv_copy = pltpu.make_async_copy(inv_hbm, inv_ref, sems.at[8])
    inv_copy.start()
    probe_copy.start()
    solve_copy.start()
    x_copy.wait()
    acc = None
    for j in range(parts):
        at = slice(j * block, (j + 1) * block)
        w1_copies[j].wait()
        pre = dot_nn(x_ref[...], w1_ref[:, at])
        hidden = (pre * jax.nn.sigmoid(pre)).astype(BF16)
        if j == 0:
            w2_copy.wait()
        part = dot_nt(hidden, w2t_ref[:, at])
        acc = part if acc is None else acc + part
    inv_copy.wait()
    scaled = (acc * inv_ref[...]).astype(BF16)
    out_ref[2 * rows :, :] = jnp.concatenate([scaled[: rows // 2], scaled[rows // 2 :]], axis=1)
    probe_copy.wait()
    solve_copy.wait()


def encode(inputs, w_first, w2t, inv_row, probes, solves):
    rows = inputs.shape[0]
    return pl.pallas_call(
        encode_body,
        in_specs=[HBM] * 6,
        out_specs=VMEM,
        out_shape=jax.ShapeDtypeStruct((2 * rows + rows // 2, probes.shape[1]), BF16),
        scratch_shapes=[
            pltpu.VMEM(inputs.shape, BF16),
            pltpu.VMEM(w_first.shape, BF16),
            pltpu.VMEM(w2t.shape, BF16),
            pltpu.VMEM(inv_row.shape, F32),
            pltpu.SemaphoreType.DMA((9,)),
        ],
        compiler_params=params(VMEM_MOST),
        name="encode",
    )(inputs, w_first, w2t, inv_row, probes, solves)


def block_parts(ref, own_rows):
    feat = ref.shape[1] // 2
    size = 2 * own_rows + own_rows // 2
    blocks = []
    for at in range(0, ref.shape[0], size):
        packed = ref[at + 2 * own_rows : at + size, :]
        u = jnp.concatenate([packed[:, :feat], packed[:, feat:]], axis=0)
        blocks.append((ref[at : at + own_rows, :], ref[at + own_rows : at + 2 * own_rows, :], u))
    return blocks


def gate_body(sizes, *refs):
    outs = refs[-1 - len(sizes) :]
    at = 0
    for size, out_ref in zip(sizes, outs):
        start = 0
        for ref in refs[at : at + size]:
            out_ref[start : start + ref.shape[0], :] = ref[...]
            start += ref.shape[0]
        at += size
    outs[-1][...] = refs[at][...]


def gate(groups, inputs, after):
    sizes = [len(group) for group in groups]
    blocks = [block for group in groups for block in group]
    shapes = [jax.ShapeDtypeStruct((sum(b.shape[0] for b in group), group[0].shape[1]), BF16) for group in groups]
    return pl.pallas_call(
        lambda *refs: gate_body(sizes, *refs),
        in_specs=[VMEM] * (len(blocks) + 1) + [ANY] * len(after),
        out_specs=(VMEM,) * (len(groups) + 1),
        out_shape=tuple(shapes) + (jax.ShapeDtypeStruct(inputs.shape, BF16),),
        compiler_params=params(),
        name="gate",
    )(*blocks, inputs, *after)


def rows_body(own_rows, count, *refs):
    row_refs, (rowa_ref, rsp_ref) = refs[:count], refs[-2:]
    blocks = [block for ref in row_refs for block in block_parts(ref, own_rows)]
    for b, (p, s, u) in enumerate(blocks):
        at = slice(b * own_rows, (b + 1) * own_rows)
        u32 = u.astype(F32)
        h = -0.5 * jnp.sum(u32 * u32, axis=1, keepdims=True)
        h1 = h.astype(BF16).astype(F32)
        h2 = (h - h1).astype(BF16).astype(F32)
        h3 = h - h1 - h2
        lane = lax.broadcasted_iota(jnp.int32, u.shape, 1)
        tail = jnp.where(lane == 0, h1, jnp.where(lane == 1, h2, jnp.where(lane == 2, h3, 0.0)))
        minus = jnp.full((own_rows, 2 * u.shape[1]), -0.5, BF16)
        rowa_ref[at, :] = jnp.concatenate([u, minus, tail.astype(BF16)], axis=1)
        rsp_ref[at, :] = jnp.concatenate([s, p], axis=1)


def group_rows(own_rows, row_blocks):
    count = len(row_blocks)
    shape = jax.ShapeDtypeStruct((lax.axis_size("kc") * own_rows, 2 * row_blocks[0].shape[1]), BF16)
    return pl.pallas_call(
        lambda *refs: rows_body(own_rows, count, *refs),
        in_specs=[VMEM] * count,
        out_specs=(VMEM, VMEM),
        out_shape=(shape, shape),
        compiler_params=params(),
        name="rows",
    )(*row_blocks)


def pair_body(own_rows, counts, first, last, rowa_ref, rsp_ref, *refs):
    col_refs, refs = refs[: len(counts)], refs[len(counts) :]
    if not first:
        v_in, m_in, s_in = refs[:3]
    if last:
        v_ref, gone_ref, keep_ref, send_ref = refs[-4:]
    else:
        v_ref, m_ref, s_ref = refs[-3:]
    probe = v_ref.shape[1]
    feat = probe // 2
    rows = rowa_ref.shape[0]
    blocks = [block for ref, n in zip(col_refs, counts) for block in block_parts(ref, own_rows)[:n]]
    group = 2
    v, m, sums = (None, None, None) if first else (v_in[...], m_in[...], s_in[...])
    for b in range(0, len(blocks), group):
        pieces = blocks[b : b + group]
        p = jnp.concatenate([q[0] for q in pieces], axis=0)
        s = jnp.concatenate([q[1] for q in pieces], axis=0)
        u = jnp.concatenate([q[2] for q in pieces], axis=0)
        u32 = u.astype(F32)
        sq = u32 * u32
        hi = sq.astype(BF16)
        lo = (sq - hi.astype(F32)).astype(BF16)
        lane = lax.broadcasted_iota(jnp.int32, u.shape, 1)
        ones = jnp.where(lane < 3, 1.0, 0.0).astype(BF16)
        kern = jnp.exp(dot_nt(rowa_ref[...], jnp.concatenate([u, hi, lo, ones], axis=1)))
        one = kern * dot_nt(rsp_ref[:, :probe], p)
        two = kern * dot_nt(rsp_ref[:, probe:], s)
        both = one + two
        lanes = both[:, :128]
        for at in range(128, both.shape[1], 128):
            lanes = lanes + both[:, at : at + 128]
        v_part = dot_nn(kern.astype(BF16), p)
        m_part = dot_nn(one.astype(BF16), u) + dot_nn(two.astype(BF16), u)
        v = v_part if v is None else v + v_part
        m = m_part if m is None else m + m_part
        sums = lanes if sums is None else sums + lanes
    if last:
        v = [v[b * own_rows : (b + 1) * own_rows] for b in range(rows // own_rows)]
        v_ref[...] = jnp.concatenate([v[0], v[1]], axis=0)
        gone_ref[...] = jnp.concatenate([v[2], v[3]], axis=0)
        t = jnp.sum(sums, axis=1, keepdims=True) * rowa_ref[:, :feat].astype(F32) - m
        t = [t[b * own_rows : (b + 1) * own_rows] for b in range(rows // own_rows)]
        keep_ref[...] = jnp.concatenate([t[0], t[1]], axis=1)
        send_ref[...] = jnp.concatenate([t[2], t[3]], axis=1)
    else:
        v_ref[...] = v
        m_ref[...] = m
        s_ref[...] = sums


def pairs(own_rows, rowa, rsp, col_blocks, counts, before, last):
    rows, cols = rowa.shape[0], sum(counts) * own_rows
    probe = col_blocks[0].shape[1]
    feat = probe // 2
    first = before is None
    operands = [rowa, rsp] + list(col_blocks) + list(before or ())
    whole = jax.ShapeDtypeStruct((rows, probe), F32)
    half = jax.ShapeDtypeStruct((rows // 2, probe), F32)
    quarter = jax.ShapeDtypeStruct((own_rows, probe), F32)
    thin = jax.ShapeDtypeStruct((rows, feat), F32)
    return pl.pallas_call(
        lambda *refs: pair_body(own_rows, counts, first, last, *refs),
        in_specs=[VMEM] * len(operands),
        out_specs=(VMEM,) * (4 if last else 3),
        out_shape=(half, half, quarter, quarter) if last else (whole, thin, jax.ShapeDtypeStruct((rows, 128), F32)),
        compiler_params=params(),
        cost_estimate=pl.CostEstimate(flops=1, bytes_accessed=2 * (rows + cols) * 384, transcendentals=0),
        name="pairs",
    )(*operands)


def selection(mine, width, share, order):
    tall, line = lax.axis_size("kr"), lax.axis_size("kc")
    at_row = lax.broadcasted_iota(jnp.int32, (mine, 1), 0)
    piece = at_row // share
    if order:
        owner_line = jnp.zeros_like(piece)
        for i, (deep_mask, tall_mask) in enumerate(order):
            target = (lax.axis_index("enc") ^ deep_mask) * tall + (lax.axis_index("kr") ^ tall_mask)
            owner_line = jnp.where(piece == i, target, owner_line)
        piece = owner_line
    owner = share * (line * piece + lax.axis_index("kc")) + at_row % share
    at_col = lax.broadcasted_iota(jnp.int32, (mine, width), 1)
    return jnp.where(at_col == owner, 1.0, 0.0).astype(BF16)


def prepare_body(share, order, xa_ref, xb_ref, w1_ref, *refs):
    slope_ref, xt_ref, ht_ref = refs[-3:]
    width, hid = w1_ref.shape
    sel = selection(xt_ref.shape[0], width, share, order)
    block = 256
    x = jnp.concatenate([xa_ref[...], xb_ref[...]], axis=0)
    xt_ref[...] = dot_nt(sel, x).astype(BF16)
    ht = None
    for j in range(hid // block):
        at = slice(j * block, (j + 1) * block)
        pre = dot_nn(x, w1_ref[:, at])
        sig = jax.nn.sigmoid(pre)
        hidden = (pre * sig).astype(BF16)
        slope_ref[:, at] = sig * (1.0 + pre * (1.0 - sig))
        part = dot_nt(sel[:, at], hidden)
        ht = part if ht is None else ht + part
    ht_ref[...] = ht.astype(BF16)


def prepare(xa, xb, w_first, share, order, after=()):
    rows = 2 * xa.shape[0]
    width, hid = w_first.shape
    thin = jax.ShapeDtypeStruct((width // lax.axis_size("kc"), rows), BF16)
    return pl.pallas_call(
        lambda *refs: prepare_body(share, order, *refs),
        in_specs=[VMEM] * 3 + [ANY] * len(after),
        out_specs=(VMEM,) * 3,
        out_shape=(jax.ShapeDtypeStruct((rows, hid), F32), thin, thin),
        compiler_params=params(),
        cost_estimate=pl.CostEstimate(flops=1, bytes_accessed=2**20, transcendentals=0),
        name="prepare",
    )(xa, xb, w_first, *after)


def finish_body(scale, term_ref, far_ref, inv_ref, *refs):
    feat = inv_ref.shape[1]
    far = far_ref[...]
    far = jnp.concatenate([far[:, feat:], far[:, :feat]], axis=1)
    inv = jnp.concatenate([inv_ref[...], inv_ref[...]], axis=1)
    refs[-1][...] = (scale * inv * (term_ref[...] + far)).astype(BF16)


def finish(scale, term, far, inv_row, after):
    return pl.pallas_call(
        lambda *refs: finish_body(scale, *refs),
        in_specs=[VMEM] * 3 + [ANY] * len(after),
        out_specs=VMEM,
        out_shape=jax.ShapeDtypeStruct(term.shape, BF16),
        compiler_params=params(),
        name="finish",
    )(term, far, inv_row, *after)


def grads_body(sizes, d_ref, e_ref, w2t_ref, slope_a, xt_a, ht_a, slope_b, xt_b, ht_b, *out_refs):
    feat, hid = w2t_ref.shape
    d, e = d_ref[...], e_ref[...]
    dfeat_a = jnp.concatenate([d[:, :feat], e[:, :feat]], axis=0)
    dfeat_b = jnp.concatenate([d[:, feat:], e[:, feat:]], axis=0)

    def store(at, part):
        start = 0
        for size, ref in zip(sizes, out_refs):
            ref[:, at] = part[start : start + size]
            start += size

    block = 256
    for j in range(hid // block):
        at = slice(j * block, (j + 1) * block)
        dpre_a = (dot_nn(dfeat_a, w2t_ref[:, at]) * slope_a[:, at]).astype(BF16)
        dpre_b = (dot_nn(dfeat_b, w2t_ref[:, at]) * slope_b[:, at]).astype(BF16)
        store(at, (dot_nn(xt_a[...], dpre_a) + dot_nn(xt_b[...], dpre_b)).astype(BF16))
    store(slice(hid, hid + feat), (dot_nn(ht_a[...], dfeat_a) + dot_nn(ht_b[...], dfeat_b)).astype(BF16))


def grads(d, e, w2t, group_a, group_b, sizes):
    feat, hid = w2t.shape
    return pl.pallas_call(
        lambda *refs: grads_body(sizes, *refs),
        in_specs=[VMEM] * 9,
        out_specs=(VMEM,) * len(sizes),
        out_shape=tuple(jax.ShapeDtypeStruct((size, hid + feat), BF16) for size in sizes),
        compiler_params=params(),
        name="grads",
    )(d, e, w2t, *group_a, *group_b)


def relay_body(count, got_ref, *refs):
    got = got_ref[...].astype(F32)
    start = 0
    for own_ref, out_ref in zip(refs[:count], refs[-count:]):
        size = own_ref.shape[0]
        out_ref[...] = (own_ref[...].astype(F32) + got[start : start + size]).astype(out_ref.dtype)
        start += size


def relay(got, own, kinds, after=()):
    return pl.pallas_call(
        lambda *refs: relay_body(len(own), *refs),
        in_specs=[VMEM] * (1 + len(own)) + [ANY] * len(after),
        out_specs=(VMEM,) * len(own),
        out_shape=tuple(jax.ShapeDtypeStruct(x.shape, kind) for x, kind in zip(own, kinds)),
        compiler_params=params(),
        name="relay",
    )(got, *own, *after)


def total_body(*refs):
    parts, (first_ref, second_ref) = refs[:-2], refs[-2:]
    total = parts[0][...].astype(F32)
    for ref in parts[1:]:
        total = total + ref[...].astype(F32)
    hid = first_ref.shape[1]
    first_ref[...] = total[:, :hid]
    second_ref[...] = total[:, hid:]


def total(parts, hid):
    share, width = parts[0].shape
    return pl.pallas_call(
        total_body,
        in_specs=[VMEM] * len(parts),
        out_specs=(VMEM, VMEM),
        out_shape=(jax.ShapeDtypeStruct((share, hid), F32), jax.ShapeDtypeStruct((share, width - hid), F32)),
        compiler_params=params(),
        name="total",
    )(*parts)


def hold_body(x_ref, *refs):
    refs[-1][...] = x_ref[...]


def hold(x, after):
    return pl.pallas_call(
        hold_body,
        in_specs=[VMEM] + [ANY] * len(after),
        out_specs=VMEM,
        out_shape=jax.ShapeDtypeStruct(x.shape, x.dtype),
        compiler_params=params(),
        name="hold",
    )(x, *after)


def local(inputs, w_first, w_second, inv_length, probes, solves):
    own_rows, width = inputs.shape
    hid, feat = w_second.shape
    probe_width = probes.shape[1]
    line, deep, tall = lax.axis_size("kc"), lax.axis_size("enc"), lax.axis_size("kr")
    lines = deep * tall
    share = width // (line * lines)
    order = [(2, 1), (3, 1), (1, 1), (0, 1), (2, 0), (3, 0), (1, 0), (0, 0)] if (deep, tall) == (4, 2) else None
    inv_row = inv_length[None, :]
    w2t = w_second.T

    own = encode(inputs, w_first, w2t, inv_row, probes, solves)
    x_core = swap(inputs, "kc", 1)
    group_a = prepare(inputs, x_core, w_first, share, order, (own,))
    far_row = swap(own, "kc", 2)
    tall_masks = range(1, tall)
    if order:
        z_two, z_one, y_own = swap(own, "enc", 2), swap(own, "enc", 1), swap(own, "kr", 1)
        z_both, row_both, held = gate(([z_one, z_two], [own, far_row]), inputs, (y_own, group_a[1]))
        core_both = swap(row_both, "kc", 1)
        calls = [
            ([row_both, y_own], [1, 1]),
            ([z_one, z_two], [1, 1]),
            ([swap(z_both, "kr", 1)], [2]),
            ([swap(z_two, "enc", 1), swap_both(own, 3, 1)], [1, 1]),
        ]
    else:
        columns = [own]
        mask = deep // 2
        while mask:
            columns = columns + [swap(block, "enc", mask) for block in columns]
            mask //= 2
        calls = [([block] + [swap(block, "kr", m) for m in tall_masks], [1] * tall) for block in columns]
        row_both, held = gate(([own, far_row],), inputs, ())
        core_both = swap(row_both, "kc", 1)
    rowa, rsp = group_rows(own_rows, [row_both, core_both])
    x_far = swap(held, "kc", 2)

    sofar = None
    for i, (blocks, counts) in enumerate(calls):
        sofar = pairs(own_rows, rowa, rsp, blocks, counts, sofar, i == len(calls) - 1)
    stay, gone, keep, send = sofar
    x_both = swap(hold(x_far, (send,)), "kc", 1)
    group_b = prepare(x_far, x_both, w_first, share, order, (send,))
    term = keep + swap(send, "kc", 1)
    lscale = loss_gain / math.sqrt(probe_width)
    dfeat = finish(-lscale, term, swap(term, "kc", 2), inv_row, (group_b[1],))
    other = swap(dfeat, "kc", 1)
    stay = stay + swap(hold(gone, (term,)), "kc", 1)
    sizes = [share * n for n in (4, 1, 1, 1, 1)] if order else [width // line]
    parts = grads(dfeat, other, w2t, group_a, group_b, sizes)
    far = swap(hold(stay[own_rows:], (parts[0],)), "kc", 2)
    if order:
        two, three, one, here = relay(swap(parts[0], "kr", 1), parts[1:], (BF16, BF16, BF16, F32), (far,))
        got = [here, swap(two, "enc", 2), swap(three, "enc", 3), swap(one, "enc", 1)]
    else:
        flat = lax.all_to_all(parts[0], ("enc", "kr"), 0, 0, tiled=True)
        got = list(flat.astype(F32).reshape(lines, share, hid + feat))
    grad_first, grad_second = total(got, hid)

    v = stay[:own_rows] + far
    products = (v * probe_gain).astype(BF16)
    return products, grad_first, grad_second


def solution(mesh):
    rows = P(("enc", "kr", "kc"), None)
    return jax.shard_map(
        local,
        mesh=mesh,
        in_specs=(rows, P(), P(), P(), rows, rows),
        out_specs=(rows, rows, rows),
        check_vma=False,
    )
```

```python
import math

import jax
import jax.numpy as jnp
from jax import lax
from jax.experimental import pallas as pl
from jax.experimental.pallas import tpu as pltpu
from jax.sharding import PartitionSpec as P

probe_gain = 0.5
loss_gain = 0.02
F32 = jnp.float32
BF16 = jnp.bfloat16
VMEM_LIMIT = 48 * 1024 * 1024
VMEM_MOST = 60 * 1024 * 1024
VMEM = pl.BlockSpec(memory_space=pltpu.VMEM)
HBM = pl.BlockSpec(memory_space=pltpu.HBM)
ANY = pl.BlockSpec(memory_space=pl.ANY)


def dot_nn(left, right):
    return lax.dot_general(left, right, (((1,), (0,)), ((), ())), preferred_element_type=F32)


def dot_nt(left, right):
    return lax.dot_general(left, right, (((1,), (1,)), ((), ())), preferred_element_type=F32)


def swap(x, axis, mask):
    size = lax.axis_size(axis)
    return lax.ppermute(x, axis, [(i, i ^ mask) for i in range(size)])


def swap_both(x, deep_mask, tall_mask):
    deep, tall = lax.axis_size("enc"), lax.axis_size("kr")
    pairs_of = [(i, ((i // tall) ^ deep_mask) * tall + ((i % tall) ^ tall_mask)) for i in range(deep * tall)]
    return lax.ppermute(x, ("enc", "kr"), pairs_of)


def params(limit=VMEM_LIMIT):
    return pltpu.CompilerParams(vmem_limit_bytes=limit)


def encode_body(x_hbm, w1_hbm, w2t_hbm, inv_hbm, probe_hbm, solve_hbm, out_ref, x_ref, w1_ref, w2t_ref, inv_ref, sems):
    rows, width = x_ref.shape
    hid = w1_ref.shape[1]
    parts = 4
    block = hid // parts
    x_copy = pltpu.make_async_copy(x_hbm, x_ref, sems.at[0])
    w2_copy = pltpu.make_async_copy(w2t_hbm, w2t_ref, sems.at[1])
    probe_copy = pltpu.make_async_copy(probe_hbm, out_ref.at[pl.ds(0, rows), :], sems.at[2])
    solve_copy = pltpu.make_async_copy(solve_hbm, out_ref.at[pl.ds(rows, rows), :], sems.at[3])
    w1_copies = [
        pltpu.make_async_copy(w1_hbm.at[:, pl.ds(j * block, block)], w1_ref.at[:, pl.ds(j * block, block)], sems.at[4 + j])
        for j in range(parts)
    ]
    x_copy.start()
    w1_copies[0].start()
    w2_copy.start()
    for copy in w1_copies[1:]:
        copy.start()
    inv_copy = pltpu.make_async_copy(inv_hbm, inv_ref, sems.at[8])
    inv_copy.start()
    probe_copy.start()
    solve_copy.start()
    x_copy.wait()
    acc = None
    for j in range(parts):
        at = slice(j * block, (j + 1) * block)
        w1_copies[j].wait()
        pre = dot_nn(x_ref[...], w1_ref[:, at])
        hidden = (pre * jax.nn.sigmoid(pre)).astype(BF16)
        if j == 0:
            w2_copy.wait()
        part = dot_nt(hidden, w2t_ref[:, at])
        acc = part if acc is None else acc + part
    inv_copy.wait()
    scaled = (acc * inv_ref[...]).astype(BF16)
    out_ref[2 * rows :, :] = jnp.concatenate([scaled[: rows // 2], scaled[rows // 2 :]], axis=1)
    probe_copy.wait()
    solve_copy.wait()


def encode(inputs, w_first, w2t, inv_row, probes, solves):
    rows = inputs.shape[0]
    return pl.pallas_call(
        encode_body,
        in_specs=[HBM] * 6,
        out_specs=VMEM,
        out_shape=jax.ShapeDtypeStruct((2 * rows + rows // 2, probes.shape[1]), BF16),
        scratch_shapes=[
            pltpu.VMEM(inputs.shape, BF16),
            pltpu.VMEM(w_first.shape, BF16),
            pltpu.VMEM(w2t.shape, BF16),
            pltpu.VMEM(inv_row.shape, F32),
            pltpu.SemaphoreType.DMA((9,)),
        ],
        compiler_params=params(VMEM_MOST),
        name="encode",
    )(inputs, w_first, w2t, inv_row, probes, solves)


def block_parts(ref, own_rows):
    feat = ref.shape[1] // 2
    size = 2 * own_rows + own_rows // 2
    blocks = []
    for at in range(0, ref.shape[0], size):
        packed = ref[at + 2 * own_rows : at + size, :]
        u = jnp.concatenate([packed[:, :feat], packed[:, feat:]], axis=0)
        blocks.append((ref[at : at + own_rows, :], ref[at + own_rows : at + 2 * own_rows, :], u))
    return blocks


def gate_body(sizes, *refs):
    outs = refs[-len(sizes) :]
    at = 0
    for size, out_ref in zip(sizes, outs):
        start = 0
        for ref in refs[at : at + size]:
            out_ref[start : start + ref.shape[0], :] = ref[...]
            start += ref.shape[0]
        at += size


def gate(groups, after=()):
    sizes = [len(group) for group in groups]
    blocks = [block for group in groups for block in group]
    shapes = [jax.ShapeDtypeStruct((sum(b.shape[0] for b in group), group[0].shape[1]), BF16) for group in groups]
    return pl.pallas_call(
        lambda *refs: gate_body(sizes, *refs),
        in_specs=[VMEM] * len(blocks) + [ANY] * len(after),
        out_specs=(VMEM,) * len(groups),
        out_shape=tuple(shapes),
        compiler_params=params(),
        name="gate",
    )(*blocks, *after)


def rows_body(own_rows, count, *refs):
    row_refs, (rowa_ref, rsp_ref) = refs[:count], refs[-2:]
    blocks = [block for ref in row_refs for block in block_parts(ref, own_rows)]
    for b, (p, s, u) in enumerate(blocks):
        at = slice(b * own_rows, (b + 1) * own_rows)
        u32 = u.astype(F32)
        h = -0.5 * jnp.sum(u32 * u32, axis=1, keepdims=True)
        h1 = h.astype(BF16).astype(F32)
        h2 = (h - h1).astype(BF16).astype(F32)
        h3 = h - h1 - h2
        lane = lax.broadcasted_iota(jnp.int32, u.shape, 1)
        tail = jnp.where(lane == 0, h1, jnp.where(lane == 1, h2, jnp.where(lane == 2, h3, 0.0)))
        minus = jnp.full((own_rows, 2 * u.shape[1]), -0.5, BF16)
        rowa_ref[at, :] = jnp.concatenate([u, minus, tail.astype(BF16)], axis=1)
        rsp_ref[at, :] = jnp.concatenate([s, p], axis=1)


def group_rows(own_rows, row_blocks):
    count = len(row_blocks)
    shape = jax.ShapeDtypeStruct((lax.axis_size("kc") * own_rows, 2 * row_blocks[0].shape[1]), BF16)
    return pl.pallas_call(
        lambda *refs: rows_body(own_rows, count, *refs),
        in_specs=[VMEM] * count,
        out_specs=(VMEM, VMEM),
        out_shape=(shape, shape),
        compiler_params=params(),
        name="rows",
    )(*row_blocks)


def pair_body(own_rows, counts, first, last, rowa_ref, rsp_ref, *refs):
    col_refs, refs = refs[: len(counts)], refs[len(counts) :]
    if not first:
        v_in, m_in, s_in = refs[:3]
    if last:
        v_ref, gone_ref, keep_ref, send_ref = refs[-4:]
    else:
        v_ref, m_ref, s_ref = refs[-3:]
    probe = v_ref.shape[1]
    feat = probe // 2
    rows = rowa_ref.shape[0]
    blocks = [block for ref, n in zip(col_refs, counts) for block in block_parts(ref, own_rows)[:n]]
    group = 2
    v, m, sums = (None, None, None) if first else (v_in[...], m_in[...], s_in[...])
    for b in range(0, len(blocks), group):
        pieces = blocks[b : b + group]
        p = jnp.concatenate([q[0] for q in pieces], axis=0)
        s = jnp.concatenate([q[1] for q in pieces], axis=0)
        u = jnp.concatenate([q[2] for q in pieces], axis=0)
        u32 = u.astype(F32)
        sq = u32 * u32
        hi = sq.astype(BF16)
        lo = (sq - hi.astype(F32)).astype(BF16)
        lane = lax.broadcasted_iota(jnp.int32, u.shape, 1)
        ones = jnp.where(lane < 3, 1.0, 0.0).astype(BF16)
        kern = jnp.exp(dot_nt(rowa_ref[...], jnp.concatenate([u, hi, lo, ones], axis=1)))
        one = kern * dot_nt(rsp_ref[:, :probe], p)
        two = kern * dot_nt(rsp_ref[:, probe:], s)
        both = one + two
        lanes = both[:, :128]
        for at in range(128, both.shape[1], 128):
            lanes = lanes + both[:, at : at + 128]
        v_part = dot_nn(kern.astype(BF16), p)
        m_part = dot_nn(one.astype(BF16), u) + dot_nn(two.astype(BF16), u)
        v = v_part if v is None else v + v_part
        m = m_part if m is None else m + m_part
        sums = lanes if sums is None else sums + lanes
    if last:
        v = [v[b * own_rows : (b + 1) * own_rows] for b in range(rows // own_rows)]
        v_ref[...] = jnp.concatenate([v[0], v[1]], axis=0)
        gone_ref[...] = jnp.concatenate([v[2], v[3]], axis=0)
        t = jnp.sum(sums, axis=1, keepdims=True) * rowa_ref[:, :feat].astype(F32) - m
        t = [t[b * own_rows : (b + 1) * own_rows] for b in range(rows // own_rows)]
        keep_ref[...] = jnp.concatenate([t[0], t[1]], axis=1)
        send_ref[...] = jnp.concatenate([t[2], t[3]], axis=1)
    else:
        v_ref[...] = v
        m_ref[...] = m
        s_ref[...] = sums


def pairs(own_rows, rowa, rsp, col_blocks, counts, before, last):
    rows, cols = rowa.shape[0], sum(counts) * own_rows
    probe = col_blocks[0].shape[1]
    feat = probe // 2
    first = before is None
    operands = [rowa, rsp] + list(col_blocks) + list(before or ())
    whole = jax.ShapeDtypeStruct((rows, probe), F32)
    half = jax.ShapeDtypeStruct((rows // 2, probe), F32)
    quarter = jax.ShapeDtypeStruct((own_rows, probe), F32)
    thin = jax.ShapeDtypeStruct((rows, feat), F32)
    return pl.pallas_call(
        lambda *refs: pair_body(own_rows, counts, first, last, *refs),
        in_specs=[VMEM] * len(operands),
        out_specs=(VMEM,) * (4 if last else 3),
        out_shape=(half, half, quarter, quarter) if last else (whole, thin, jax.ShapeDtypeStruct((rows, 128), F32)),
        compiler_params=params(),
        cost_estimate=pl.CostEstimate(flops=1, bytes_accessed=2 * (rows + cols) * 384, transcendentals=0),
        name="pairs",
    )(*operands)


def selection(mine, width, share, order):
    tall, line = lax.axis_size("kr"), lax.axis_size("kc")
    at_row = lax.broadcasted_iota(jnp.int32, (mine, 1), 0)
    piece = at_row // share
    if order:
        owner_line = jnp.zeros_like(piece)
        for i, (deep_mask, tall_mask) in enumerate(order):
            target = (lax.axis_index("enc") ^ deep_mask) * tall + (lax.axis_index("kr") ^ tall_mask)
            owner_line = jnp.where(piece == i, target, owner_line)
        piece = owner_line
    owner = share * (line * piece + lax.axis_index("kc")) + at_row % share
    at_col = lax.broadcasted_iota(jnp.int32, (mine, width), 1)
    return jnp.where(at_col == owner, 1.0, 0.0).astype(BF16)


def prepare_body(share, order, xa_ref, xb_ref, w1_ref, *refs):
    slope_ref, xt_ref, ht_ref = refs[-3:]
    width, hid = w1_ref.shape
    sel = selection(xt_ref.shape[0], width, share, order)
    block = 256
    x = jnp.concatenate([xa_ref[...], xb_ref[...]], axis=0)
    xt_ref[...] = dot_nt(sel, x).astype(BF16)
    ht = None
    for j in range(hid // block):
        at = slice(j * block, (j + 1) * block)
        pre = dot_nn(x, w1_ref[:, at])
        sig = jax.nn.sigmoid(pre)
        hidden = (pre * sig).astype(BF16)
        slope_ref[:, at] = sig * (1.0 + pre * (1.0 - sig))
        part = dot_nt(sel[:, at], hidden)
        ht = part if ht is None else ht + part
    ht_ref[...] = ht.astype(BF16)


def prepare(xa, xb, w_first, share, order, after):
    rows = 2 * xa.shape[0]
    width, hid = w_first.shape
    thin = jax.ShapeDtypeStruct((width // lax.axis_size("kc"), rows), BF16)
    return pl.pallas_call(
        lambda *refs: prepare_body(share, order, *refs),
        in_specs=[VMEM] * 3 + [ANY] * len(after),
        out_specs=(VMEM,) * 3,
        out_shape=(jax.ShapeDtypeStruct((rows, hid), F32), thin, thin),
        compiler_params=params(),
        cost_estimate=pl.CostEstimate(flops=1, bytes_accessed=2**20, transcendentals=0),
        name="prepare",
    )(xa, xb, w_first, *after)


def finish_body(scale, term_ref, far_ref, inv_ref, *refs):
    feat = inv_ref.shape[1]
    far = far_ref[...]
    far = jnp.concatenate([far[:, feat:], far[:, :feat]], axis=1)
    inv = jnp.concatenate([inv_ref[...], inv_ref[...]], axis=1)
    refs[-1][...] = (scale * inv * (term_ref[...] + far)).astype(BF16)


def finish(scale, term, far, inv_row, after):
    return pl.pallas_call(
        lambda *refs: finish_body(scale, *refs),
        in_specs=[VMEM] * 3 + [ANY] * len(after),
        out_specs=VMEM,
        out_shape=jax.ShapeDtypeStruct(term.shape, BF16),
        compiler_params=params(),
        name="finish",
    )(term, far, inv_row, *after)


def grads_body(sizes, d_ref, e_ref, w2t_ref, slope_a, xt_a, ht_a, slope_b, xt_b, ht_b, *out_refs):
    feat, hid = w2t_ref.shape
    d, e = d_ref[...], e_ref[...]
    dfeat_a = jnp.concatenate([d[:, :feat], e[:, :feat]], axis=0)
    dfeat_b = jnp.concatenate([d[:, feat:], e[:, feat:]], axis=0)

    def store(at, part):
        start = 0
        for size, ref in zip(sizes, out_refs):
            ref[:, at] = part[start : start + size]
            start += size

    block = 256
    for j in range(hid // block):
        at = slice(j * block, (j + 1) * block)
        dpre_a = (dot_nn(dfeat_a, w2t_ref[:, at]) * slope_a[:, at]).astype(BF16)
        dpre_b = (dot_nn(dfeat_b, w2t_ref[:, at]) * slope_b[:, at]).astype(BF16)
        store(at, (dot_nn(xt_a[...], dpre_a) + dot_nn(xt_b[...], dpre_b)).astype(BF16))
    store(slice(hid, hid + feat), (dot_nn(ht_a[...], dfeat_a) + dot_nn(ht_b[...], dfeat_b)).astype(BF16))


def grads(d, e, w2t, group_a, group_b, sizes):
    feat, hid = w2t.shape
    return pl.pallas_call(
        lambda *refs: grads_body(sizes, *refs),
        in_specs=[VMEM] * 9,
        out_specs=(VMEM,) * len(sizes),
        out_shape=tuple(jax.ShapeDtypeStruct((size, hid + feat), BF16) for size in sizes),
        compiler_params=params(),
        name="grads",
    )(d, e, w2t, *group_a, *group_b)


def relay_body(count, got_ref, *refs):
    got = got_ref[...].astype(F32)
    start = 0
    for own_ref, out_ref in zip(refs[:count], refs[-count:]):
        size = own_ref.shape[0]
        out_ref[...] = (own_ref[...].astype(F32) + got[start : start + size]).astype(out_ref.dtype)
        start += size


def relay(got, own, kinds, after=()):
    return pl.pallas_call(
        lambda *refs: relay_body(len(own), *refs),
        in_specs=[VMEM] * (1 + len(own)) + [ANY] * len(after),
        out_specs=(VMEM,) * len(own),
        out_shape=tuple(jax.ShapeDtypeStruct(x.shape, kind) for x, kind in zip(own, kinds)),
        compiler_params=params(),
        name="relay",
    )(got, *own, *after)


def total_body(*refs):
    parts, (first_ref, second_ref) = refs[:-2], refs[-2:]
    total = parts[0][...].astype(F32)
    for ref in parts[1:]:
        total = total + ref[...].astype(F32)
    hid = first_ref.shape[1]
    first_ref[...] = total[:, :hid]
    second_ref[...] = total[:, hid:]


def total(parts, hid):
    share, width = parts[0].shape
    return pl.pallas_call(
        total_body,
        in_specs=[VMEM] * len(parts),
        out_specs=(VMEM, VMEM),
        out_shape=(jax.ShapeDtypeStruct((share, hid), F32), jax.ShapeDtypeStruct((share, width - hid), F32)),
        compiler_params=params(),
        name="total",
    )(*parts)


def hold_body(x_ref, *refs):
    refs[-1][...] = x_ref[...]


def hold(x, after):
    return pl.pallas_call(
        hold_body,
        in_specs=[VMEM] + [ANY] * len(after),
        out_specs=VMEM,
        out_shape=jax.ShapeDtypeStruct(x.shape, x.dtype),
        compiler_params=params(),
        name="hold",
    )(x, *after)


def local(inputs, w_first, w_second, inv_length, probes, solves):
    own_rows, width = inputs.shape
    hid, feat = w_second.shape
    probe_width = probes.shape[1]
    line, deep, tall = lax.axis_size("kc"), lax.axis_size("enc"), lax.axis_size("kr")
    lines = deep * tall
    share = width // (line * lines)
    order = [(2, 1), (3, 1), (1, 1), (2, 0), (3, 0), (1, 0), (0, 1), (0, 0)] if (deep, tall) == (4, 2) else None
    inv_row = inv_length[None, :]
    w2t = w_second.T

    own = encode(inputs, w_first, w2t, inv_row, probes, solves)
    x_core = swap(inputs, "kc", 1)
    group_a = prepare(inputs, x_core, w_first, share, order, (own,))
    far_row = swap(own, "kc", 2)
    tall_masks = range(1, tall)
    if order:
        z_two, z_one, y_own = swap(own, "enc", 2), swap(own, "enc", 1), swap(own, "kr", 1)
        z_both, row_both = gate(([z_one, z_two], [own, far_row]), (y_own, group_a[1]))
        core_both = swap(row_both, "kc", 1)
        calls = [
            ([row_both, y_own], [1, 1]),
            ([z_one, z_two], [1, 1]),
            ([swap(z_both, "kr", 1)], [2]),
            ([swap(z_two, "enc", 1), swap(y_own, "enc", 3)], [1, 1]),
        ]
    else:
        columns = [own]
        mask = deep // 2
        while mask:
            columns = columns + [swap(block, "enc", mask) for block in columns]
            mask //= 2
        calls = [([block] + [swap(block, "kr", m) for m in tall_masks], [1] * tall) for block in columns]
        (row_both,) = gate(([own, far_row],))
        core_both = swap(row_both, "kc", 1)
    rowa, rsp = group_rows(own_rows, [row_both, core_both])
    x_far = swap(hold(inputs, (core_both,)), "kc", 2)

    sofar = None
    for i, (blocks, counts) in enumerate(calls):
        sofar = pairs(own_rows, rowa, rsp, blocks, counts, sofar, i == len(calls) - 1)
    stay, gone, keep, send = sofar
    term = keep + swap(send, "kc", 1)
    x_both = swap(hold(x_far, (term,)), "kc", 1)
    group_b = prepare(x_far, x_both, w_first, share, order, (send,))
    lscale = loss_gain / math.sqrt(probe_width)
    dfeat = finish(-lscale, term, swap(term, "kc", 2), inv_row, (group_b[1],))
    other = swap(dfeat, "kc", 1)
    stay = stay + swap(hold(gone, (term,)), "kc", 1)
    sizes = [share * n for n in (3, 1, 1, 1, 1, 1)] if order else [width // line]
    parts = grads(dfeat, other, w2t, group_a, group_b, sizes)
    far = swap(hold(stay[own_rows:], (parts[0],)), "kc", 2)
    if order:
        two, three, one = relay(swap(parts[0], "kr", 1), parts[1:4], (BF16,) * 3, (far,))
        got = [parts[5], swap(two, "enc", 2), swap(three, "enc", 3), swap(one, "enc", 1), swap(parts[4], "kr", 1)]
    else:
        flat = lax.all_to_all(parts[0], ("enc", "kr"), 0, 0, tiled=True)
        got = list(flat.astype(F32).reshape(lines, share, hid + feat))
    grad_first, grad_second = total(got, hid)

    v = stay[:own_rows] + far
    products = (v * probe_gain).astype(BF16)
    return products, grad_first, grad_second


def solution(mesh):
    rows = P(("enc", "kr", "kc"), None)
    return jax.shard_map(
        local,
        mesh=mesh,
        in_specs=(rows, P(), P(), P(), rows, rows),
        out_specs=(rows, rows, rows),
        check_vma=False,
    )
```

```python
import math

import jax
import jax.numpy as jnp
from jax import lax
from jax.experimental import pallas as pl
from jax.experimental.pallas import tpu as pltpu
from jax.sharding import PartitionSpec as P

probe_gain = 0.5
loss_gain = 0.02
F32 = jnp.float32
BF16 = jnp.bfloat16
VMEM_LIMIT = 48 * 1024 * 1024
VMEM_MOST = 58 * 1024 * 1024
VMEM = pl.BlockSpec(memory_space=pltpu.VMEM)
HBM = pl.BlockSpec(memory_space=pltpu.HBM)
ANY = pl.BlockSpec(memory_space=pl.ANY)


def dot_nn(left, right):
    return lax.dot_general(left, right, (((1,), (0,)), ((), ())), preferred_element_type=F32)


def dot_nt(left, right):
    return lax.dot_general(left, right, (((1,), (1,)), ((), ())), preferred_element_type=F32)


def swap(x, axis, mask):
    size = lax.axis_size(axis)
    return lax.ppermute(x, axis, [(i, i ^ mask) for i in range(size)])


def swap_both(x, deep_mask, tall_mask):
    deep, tall = lax.axis_size("enc"), lax.axis_size("kr")
    pairs_of = [(i, ((i // tall) ^ deep_mask) * tall + ((i % tall) ^ tall_mask)) for i in range(deep * tall)]
    return lax.ppermute(x, ("enc", "kr"), pairs_of)


def params(limit=VMEM_LIMIT):
    return pltpu.CompilerParams(vmem_limit_bytes=limit)


def encode_body(x_hbm, w1_hbm, w2t_hbm, inv_hbm, probe_hbm, solve_hbm, out_ref, x_ref, w1_ref, w2t_ref, inv_ref, sems):
    rows, width = x_ref.shape
    hid = w1_ref.shape[1]
    parts = 2
    block = hid // parts
    x_copy = pltpu.make_async_copy(x_hbm, x_ref, sems.at[0])
    w2_copy = pltpu.make_async_copy(w2t_hbm, w2t_ref, sems.at[1])
    probe_copy = pltpu.make_async_copy(probe_hbm, out_ref.at[pl.ds(0, rows), :], sems.at[2])
    solve_copy = pltpu.make_async_copy(solve_hbm, out_ref.at[pl.ds(rows, rows), :], sems.at[3])
    w1_copies = [
        pltpu.make_async_copy(w1_hbm.at[:, pl.ds(j * block, block)], w1_ref.at[:, pl.ds(j * block, block)], sems.at[4 + j])
        for j in range(parts)
    ]
    x_copy.start()
    w1_copies[0].start()
    w2_copy.start()
    for copy in w1_copies[1:]:
        copy.start()
    inv_copy = pltpu.make_async_copy(inv_hbm, inv_ref, sems.at[8])
    inv_copy.start()
    probe_copy.start()
    solve_copy.start()
    x_copy.wait()
    acc = None
    for j in range(parts):
        at = slice(j * block, (j + 1) * block)
        w1_copies[j].wait()
        pre = dot_nn(x_ref[...], w1_ref[:, at])
        hidden = (pre * jax.nn.sigmoid(pre)).astype(BF16)
        if j == 0:
            w2_copy.wait()
        part = dot_nt(hidden, w2t_ref[:, at])
        acc = part if acc is None else acc + part
    inv_copy.wait()
    scaled = (acc * inv_ref[...]).astype(BF16)
    out_ref[2 * rows :, :] = jnp.concatenate([scaled[: rows // 2], scaled[rows // 2 :]], axis=1)
    probe_copy.wait()
    solve_copy.wait()


def encode(inputs, w_first, w2t, inv_row, probes, solves):
    rows = inputs.shape[0]
    return pl.pallas_call(
        encode_body,
        in_specs=[HBM] * 6,
        out_specs=VMEM,
        out_shape=jax.ShapeDtypeStruct((2 * rows + rows // 2, probes.shape[1]), BF16),
        scratch_shapes=[
            pltpu.VMEM(inputs.shape, BF16),
            pltpu.VMEM(w_first.shape, BF16),
            pltpu.VMEM(w2t.shape, BF16),
            pltpu.VMEM(inv_row.shape, F32),
            pltpu.SemaphoreType.DMA((9,)),
        ],
        compiler_params=params(VMEM_MOST),
        name="encode",
    )(inputs, w_first, w2t, inv_row, probes, solves)


def block_parts(ref, own_rows):
    feat = ref.shape[1] // 2
    size = 2 * own_rows + own_rows // 2
    blocks = []
    for at in range(0, ref.shape[0], size):
        packed = ref[at + 2 * own_rows : at + size, :]
        u = jnp.concatenate([packed[:, :feat], packed[:, feat:]], axis=0)
        blocks.append((ref[at : at + own_rows, :], ref[at + own_rows : at + 2 * own_rows, :], u))
    return blocks


def gate_body(sizes, *refs):
    outs = refs[-len(sizes) :]
    at = 0
    for size, out_ref in zip(sizes, outs):
        start = 0
        for ref in refs[at : at + size]:
            out_ref[start : start + ref.shape[0], :] = ref[...]
            start += ref.shape[0]
        at += size


def gate(groups, after=()):
    sizes = [len(group) for group in groups]
    blocks = [block for group in groups for block in group]
    shapes = [jax.ShapeDtypeStruct((sum(b.shape[0] for b in group), group[0].shape[1]), BF16) for group in groups]
    return pl.pallas_call(
        lambda *refs: gate_body(sizes, *refs),
        in_specs=[VMEM] * len(blocks) + [ANY] * len(after),
        out_specs=(VMEM,) * len(groups),
        out_shape=tuple(shapes),
        compiler_params=params(),
        name="gate",
    )(*blocks, *after)


def rows_body(own_rows, count, *refs):
    row_refs, (rowa_ref, rsp_ref) = refs[:count], refs[-2:]
    blocks = [block for ref in row_refs for block in block_parts(ref, own_rows)]
    for b, (p, s, u) in enumerate(blocks):
        at = slice(b * own_rows, (b + 1) * own_rows)
        u32 = u.astype(F32)
        h = -0.5 * jnp.sum(u32 * u32, axis=1, keepdims=True)
        h1 = h.astype(BF16).astype(F32)
        h2 = (h - h1).astype(BF16).astype(F32)
        h3 = h - h1 - h2
        lane = lax.broadcasted_iota(jnp.int32, u.shape, 1)
        tail = jnp.where(lane == 0, h1, jnp.where(lane == 1, h2, jnp.where(lane == 2, h3, 0.0)))
        minus = jnp.full((own_rows, 2 * u.shape[1]), -0.5, BF16)
        rowa_ref[at, :] = jnp.concatenate([u, minus, tail.astype(BF16)], axis=1)
        rsp_ref[at, :] = jnp.concatenate([s, p], axis=1)


def group_rows(own_rows, row_blocks):
    count = len(row_blocks)
    shape = jax.ShapeDtypeStruct((lax.axis_size("kc") * own_rows, 2 * row_blocks[0].shape[1]), BF16)
    return pl.pallas_call(
        lambda *refs: rows_body(own_rows, count, *refs),
        in_specs=[VMEM] * count,
        out_specs=(VMEM, VMEM),
        out_shape=(shape, shape),
        compiler_params=params(),
        name="rows",
    )(*row_blocks)


def pair_body(own_rows, counts, first, last, rowa_ref, rsp_ref, *refs):
    col_refs, refs = refs[: len(counts)], refs[len(counts) :]
    if not first:
        v_in, m_in, s_in = refs[:3]
    if last:
        v_ref, gone_ref, term_ref = refs[-3:]
    else:
        v_ref, m_ref, s_ref = refs[-3:]
    probe = v_ref.shape[1]
    feat = probe // 2
    rows = rowa_ref.shape[0]
    blocks = [block for ref, n in zip(col_refs, counts) for block in block_parts(ref, own_rows)[:n]]
    group = 2
    v, m, sums = (None, None, None) if first else (v_in[...], m_in[...], s_in[...])
    for b in range(0, len(blocks), group):
        pieces = blocks[b : b + group]
        p = jnp.concatenate([q[0] for q in pieces], axis=0)
        s = jnp.concatenate([q[1] for q in pieces], axis=0)
        u = jnp.concatenate([q[2] for q in pieces], axis=0)
        u32 = u.astype(F32)
        sq = u32 * u32
        hi = sq.astype(BF16)
        lo = (sq - hi.astype(F32)).astype(BF16)
        lane = lax.broadcasted_iota(jnp.int32, u.shape, 1)
        ones = jnp.where(lane < 3, 1.0, 0.0).astype(BF16)
        kern = jnp.exp(dot_nt(rowa_ref[...], jnp.concatenate([u, hi, lo, ones], axis=1)))
        one = kern * dot_nt(rsp_ref[:, :probe], p)
        two = kern * dot_nt(rsp_ref[:, probe:], s)
        both = one + two
        lanes = both[:, :128]
        for at in range(128, both.shape[1], 128):
            lanes = lanes + both[:, at : at + 128]
        v_part = dot_nn(kern.astype(BF16), p)
        m_part = dot_nn(one.astype(BF16), u) + dot_nn(two.astype(BF16), u)
        v = v_part if v is None else v + v_part
        m = m_part if m is None else m + m_part
        sums = lanes if sums is None else sums + lanes
    if last:
        v = [v[b * own_rows : (b + 1) * own_rows] for b in range(rows // own_rows)]
        v_ref[...] = jnp.concatenate([v[0], v[1]], axis=0)
        gone_ref[...] = jnp.concatenate([v[2], v[3]], axis=0)
        t = jnp.sum(sums, axis=1, keepdims=True) * rowa_ref[:, :feat].astype(F32) - m
        t = [t[b * own_rows : (b + 1) * own_rows] for b in range(rows // own_rows)]
        term_ref[:own_rows, :] = jnp.concatenate([t[0], t[1]], axis=1)
        term_ref[own_rows:, :] = jnp.concatenate([t[2], t[3]], axis=1)
    else:
        v_ref[...] = v
        m_ref[...] = m
        s_ref[...] = sums


def pairs(own_rows, rowa, rsp, col_blocks, counts, before, last):
    rows, cols = rowa.shape[0], sum(counts) * own_rows
    probe = col_blocks[0].shape[1]
    feat = probe // 2
    first = before is None
    operands = [rowa, rsp] + list(col_blocks) + list(before or ())
    whole = jax.ShapeDtypeStruct((rows, probe), F32)
    half = jax.ShapeDtypeStruct((rows // 2, probe), F32)
    thin = jax.ShapeDtypeStruct((rows, feat), F32)
    return pl.pallas_call(
        lambda *refs: pair_body(own_rows, counts, first, last, *refs),
        in_specs=[VMEM] * len(operands),
        out_specs=(VMEM,) * 3,
        out_shape=(half, half, half) if last else (whole, thin, jax.ShapeDtypeStruct((rows, 128), F32)),
        compiler_params=params(),
        cost_estimate=pl.CostEstimate(flops=1, bytes_accessed=2 * (rows + cols) * 384, transcendentals=0),
        name="pairs",
    )(*operands)


def selection(mine, width, share, order):
    tall, line = lax.axis_size("kr"), lax.axis_size("kc")
    at_row = lax.broadcasted_iota(jnp.int32, (mine, 1), 0)
    piece = at_row // share
    if order:
        owner_line = jnp.zeros_like(piece)
        for i, (deep_mask, tall_mask) in enumerate(order):
            target = (lax.axis_index("enc") ^ deep_mask) * tall + (lax.axis_index("kr") ^ tall_mask)
            owner_line = jnp.where(piece == i, target, owner_line)
        piece = owner_line
    owner = share * (line * piece + lax.axis_index("kc")) + at_row % share
    at_col = lax.broadcasted_iota(jnp.int32, (mine, width), 1)
    return jnp.where(at_col == owner, 1.0, 0.0).astype(BF16)


def prepare_body(share, order, xa_ref, xb_ref, w1_ref, *refs):
    slope_ref, xt_ref, ht_ref = refs[-3:]
    width, hid = w1_ref.shape
    sel = selection(xt_ref.shape[0], width, share, order)
    block = 256
    x = jnp.concatenate([xa_ref[...], xb_ref[...]], axis=0)
    xt_ref[...] = dot_nt(sel, x).astype(BF16)
    ht = None
    for j in range(hid // block):
        at = slice(j * block, (j + 1) * block)
        pre = dot_nn(x, w1_ref[:, at])
        sig = jax.nn.sigmoid(pre)
        hidden = (pre * sig).astype(BF16)
        slope_ref[:, at] = sig * (1.0 + pre * (1.0 - sig))
        part = dot_nt(sel[:, at], hidden)
        ht = part if ht is None else ht + part
    ht_ref[...] = ht.astype(BF16)


def prepare(xa, xb, w_first, share, order, after):
    rows = 2 * xa.shape[0]
    width, hid = w_first.shape
    thin = jax.ShapeDtypeStruct((width // lax.axis_size("kc"), rows), BF16)
    return pl.pallas_call(
        lambda *refs: prepare_body(share, order, *refs),
        in_specs=[VMEM] * 3 + [ANY] * len(after),
        out_specs=(VMEM,) * 3,
        out_shape=(jax.ShapeDtypeStruct((rows, hid), F32), thin, thin),
        compiler_params=params(),
        cost_estimate=pl.CostEstimate(flops=1, bytes_accessed=2**20, transcendentals=0),
        name="prepare",
    )(xa, xb, w_first, *after)


def merge_body(term_ref, got_ref, sum_ref, out_ref):
    rows = term_ref.shape[0] // 2
    feat = term_ref.shape[1] // 2
    for at, theirs in ((0, rows), (rows, 0)):
        both = term_ref[at : at + rows, :] + got_ref[theirs : theirs + rows, :]
        sum_ref[at : at + rows, :] = both
        out_ref[at : at + rows, :] = jnp.concatenate([both[:, feat:], both[:, :feat]], axis=1).astype(BF16)


def merge(term, got):
    return pl.pallas_call(
        merge_body,
        in_specs=[VMEM] * 2,
        out_specs=(VMEM, VMEM),
        out_shape=(jax.ShapeDtypeStruct(got.shape, F32), jax.ShapeDtypeStruct(got.shape, BF16)),
        compiler_params=params(),
        name="merge",
    )(term, got)


def finish_body(scale, term_ref, far_ref, inv_ref, *refs):
    inv = jnp.concatenate([inv_ref[...], inv_ref[...]], axis=1)
    refs[-1][...] = (scale * inv * (term_ref[...] + far_ref[...].astype(F32))).astype(BF16)


def finish(scale, term, far, inv_row, after):
    return pl.pallas_call(
        lambda *refs: finish_body(scale, *refs),
        in_specs=[VMEM] * 3 + [ANY] * len(after),
        out_specs=VMEM,
        out_shape=jax.ShapeDtypeStruct(term.shape, BF16),
        compiler_params=params(),
        name="finish",
    )(term, far, inv_row, *after)


def grads_body(pieces, share, d_ref, w2t_ref, slope_a, xt_a, ht_a, slope_b, xt_b, ht_b, *out_refs):
    feat, hid = w2t_ref.shape
    half = d_ref.shape[0] // 2
    d, e = d_ref[:half, :], d_ref[half:, :]
    dfeat_a = jnp.concatenate([d[:, :feat], e[:, :feat]], axis=0)
    dfeat_b = jnp.concatenate([d[:, feat:], e[:, feat:]], axis=0)
    size = dense_rows(share, hid, feat)

    def store(at, part):
        if pieces is None:
            out_refs[0][:, at : at + part.shape[1]] = part
            return
        row = 0
        for count, ref in zip(pieces, out_refs):
            for n in range(count):
                block = part[row : row + share]
                to = n * size + at * share // 128
                if at < hid:
                    for lane in range(0, part.shape[1], 128):
                        ref[to : to + share, :] = block[:, lane : lane + 128]
                        to += share
                else:
                    half = share // 2
                    ref[to : to + half, :] = jnp.concatenate([block[:half], block[half:]], axis=1)
                row += share

    width = 256
    for at in range(0, hid, width):
        cols = slice(at, at + width)
        dpre_a = (dot_nn(dfeat_a, w2t_ref[:, cols]) * slope_a[:, cols]).astype(BF16)
        dpre_b = (dot_nn(dfeat_b, w2t_ref[:, cols]) * slope_b[:, cols]).astype(BF16)
        store(at, (dot_nn(xt_a[...], dpre_a) + dot_nn(xt_b[...], dpre_b)).astype(BF16))
    store(hid, (dot_nn(ht_a[...], dfeat_a) + dot_nn(ht_b[...], dfeat_b)).astype(BF16))


def dense_rows(share, hid, feat):
    return share * (hid + feat) // 128


def grads(dfeat, w2t, group_a, group_b, pieces, share):
    feat, hid = w2t.shape
    size = dense_rows(share, hid, feat)
    shapes = [(group_a[1].shape[0], hid + feat)] if pieces is None else [(count * size, 128) for count in pieces]
    return pl.pallas_call(
        lambda *refs: grads_body(pieces, share, *refs),
        in_specs=[VMEM] * 8,
        out_specs=(VMEM,) * len(shapes),
        out_shape=tuple(jax.ShapeDtypeStruct(shape, BF16) for shape in shapes),
        compiler_params=params(),
        name="grads",
    )(dfeat, w2t, *group_a, *group_b)


def relay_body(count, got_ref, *refs):
    got = got_ref[...].astype(F32)
    start = 0
    for own_ref, out_ref in zip(refs[:count], refs[-count:]):
        size = own_ref.shape[0]
        out_ref[...] = (own_ref[...].astype(F32) + got[start : start + size]).astype(out_ref.dtype)
        start += size


def relay(got, own, kinds, after=()):
    return pl.pallas_call(
        lambda *refs: relay_body(len(own), *refs),
        in_specs=[VMEM] * (1 + len(own)) + [ANY] * len(after),
        out_specs=(VMEM,) * len(own),
        out_shape=tuple(jax.ShapeDtypeStruct(x.shape, kind) for x, kind in zip(own, kinds)),
        compiler_params=params(),
        name="relay",
    )(got, *own, *after)


def total_body(dense, *refs):
    parts, (first_ref, second_ref) = refs[:-2], refs[-2:]
    total = parts[0][...].astype(F32)
    for ref in parts[1:]:
        total = total + ref[...].astype(F32)
    share, hid = first_ref.shape
    feat = second_ref.shape[1]
    if not dense:
        first_ref[...] = total[:, :hid]
        second_ref[...] = total[:, hid:]
        return
    row = 0
    for at in range(0, hid, 128):
        first_ref[:, at : at + 128] = total[row : row + share]
        row += share
    second_ref[: share // 2, :] = total[row:, :feat]
    second_ref[share // 2 :, :] = total[row:, feat:]


def total(parts, share, hid, feat, dense):
    return pl.pallas_call(
        lambda *refs: total_body(dense, *refs),
        in_specs=[VMEM] * len(parts),
        out_specs=(VMEM, VMEM),
        out_shape=(jax.ShapeDtypeStruct((share, hid), F32), jax.ShapeDtypeStruct((share, feat), F32)),
        compiler_params=params(),
        name="total",
    )(*parts)


def hold_body(x_ref, *refs):
    refs[-1][...] = x_ref[...]


def hold(x, after):
    return pl.pallas_call(
        hold_body,
        in_specs=[VMEM] + [ANY] * len(after),
        out_specs=VMEM,
        out_shape=jax.ShapeDtypeStruct(x.shape, x.dtype),
        compiler_params=params(),
        name="hold",
    )(x, *after)


def local(inputs, w_first, w_second, inv_length, probes, solves):
    own_rows, width = inputs.shape
    hid, feat = w_second.shape
    probe_width = probes.shape[1]
    line, deep, tall = lax.axis_size("kc"), lax.axis_size("enc"), lax.axis_size("kr")
    lines = deep * tall
    share = width // (line * lines)
    order = [(2, 1), (3, 1), (1, 1), (0, 1), (2, 0), (3, 0), (1, 0), (0, 0)] if (deep, tall) == (4, 2) else None
    inv_row = inv_length[None, :]
    w2t = w_second.T

    own = encode(inputs, w_first, w2t, inv_row, probes, solves)
    x_core = swap(inputs, "kc", 1)
    group_a = prepare(inputs, x_core, w_first, share, order, (own,))
    far_row = swap(own, "kc", 2)
    tall_masks = range(1, tall)
    if order:
        z_two, z_one, y_own = swap(own, "enc", 2), swap(own, "enc", 1), swap(own, "kr", 1)
        (z_both,) = gate(([z_one, z_two],), (y_own, group_a[1]))
        (row_both,) = gate(([own, far_row],), (z_both,))
        core_both = swap(row_both, "kc", 1)
        calls = [
            ([row_both, y_own], [1, 1]),
            ([z_one, z_two], [1, 1]),
            ([swap(z_both, "kr", 1)], [2]),
            ([swap(z_two, "enc", 1), swap(y_own, "enc", 3)], [1, 1]),
        ]
    else:
        columns = [own]
        mask = deep // 2
        while mask:
            columns = columns + [swap(block, "enc", mask) for block in columns]
            mask //= 2
        calls = [([block] + [swap(block, "kr", m) for m in tall_masks], [1] * tall) for block in columns]
        (row_both,) = gate(([own, far_row],))
        core_both = swap(row_both, "kc", 1)
    rowa, rsp = group_rows(own_rows, [row_both, core_both])
    x_far = swap(inputs, "kc", 2)

    sofar = None
    for i, (blocks, counts) in enumerate(calls):
        sofar = pairs(own_rows, rowa, rsp, blocks, counts, sofar, i == len(calls) - 1)
    stay, gone, term = sofar
    term, moved = merge(term, swap(term, "kc", 1))
    x_both = swap(hold(x_far, (term,)), "kc", 1)
    group_b = prepare(x_far, x_both, w_first, share, order, (term,))
    lscale = loss_gain / math.sqrt(probe_width)
    dfeat = finish(-lscale, term, swap(moved, "kc", 2), inv_row, (group_b[1],))
    stay = stay + swap(hold(gone, (term,)), "kc", 1)
    parts = grads(dfeat, w2t, group_a, group_b, (2, 1, 1, 1, 1, 1, 1) if order else None, share)
    far = swap(hold(stay[own_rows:], (parts[0],)), "kc", 2)
    if order:
        two, three = relay(swap(parts[0], "kr", 1), parts[3:5], (BF16, BF16))
        (one,) = relay(swap(parts[1], "kr", 1), parts[5:6], (BF16,), (two, far))
        got = [parts[6], swap(two, "enc", 2), swap(three, "enc", 3), swap(one, "enc", 1), swap(parts[2], "kr", 1)]
    else:
        flat = lax.all_to_all(parts[0], ("enc", "kr"), 0, 0, tiled=True)
        got = list(flat.astype(F32).reshape(lines, share, hid + feat))
    grad_first, grad_second = total(got, share, hid, feat, order is not None)

    v = stay[:own_rows] + far
    products = (v * probe_gain).astype(BF16)
    return products, grad_first, grad_second


def solution(mesh):
    rows = P(("enc", "kr", "kc"), None)
    return jax.shard_map(
        local,
        mesh=mesh,
        in_specs=(rows, P(), P(), P(), rows, rows),
        out_specs=(rows, rows, rows),
        check_vma=False,
    )
```

```python
import math

import jax
import jax.numpy as jnp
from jax import lax
from jax.experimental import pallas as pl
from jax.experimental.pallas import tpu as pltpu
from jax.sharding import PartitionSpec as P

probe_gain = 0.5
loss_gain = 0.02
F32 = jnp.float32
BF16 = jnp.bfloat16
VMEM_LIMIT = 48 * 1024 * 1024
VMEM_MOST = 58 * 1024 * 1024
VMEM = pl.BlockSpec(memory_space=pltpu.VMEM)
HBM = pl.BlockSpec(memory_space=pltpu.HBM)
ANY = pl.BlockSpec(memory_space=pl.ANY)


def dot_nn(left, right):
    return lax.dot_general(left, right, (((1,), (0,)), ((), ())), preferred_element_type=F32)


def dot_nt(left, right):
    return lax.dot_general(left, right, (((1,), (1,)), ((), ())), preferred_element_type=F32)


def swap(x, axis, mask):
    size = lax.axis_size(axis)
    return lax.ppermute(x, axis, [(i, i ^ mask) for i in range(size)])


def swap_both(x, deep_mask, tall_mask):
    deep, tall = lax.axis_size("enc"), lax.axis_size("kr")
    pairs_of = [(i, ((i // tall) ^ deep_mask) * tall + ((i % tall) ^ tall_mask)) for i in range(deep * tall)]
    return lax.ppermute(x, ("enc", "kr"), pairs_of)


def params(limit=VMEM_LIMIT):
    return pltpu.CompilerParams(vmem_limit_bytes=limit)


def encode_body(x_hbm, w1_hbm, w2t_hbm, inv_hbm, probe_hbm, solve_hbm, out_ref, x_ref, w1_ref, w2t_ref, inv_ref, sems):
    rows, width = x_ref.shape
    hid = w1_ref.shape[1]
    parts = 2
    block = hid // parts
    x_copy = pltpu.make_async_copy(x_hbm, x_ref, sems.at[0])
    w2_copy = pltpu.make_async_copy(w2t_hbm, w2t_ref, sems.at[1])
    probe_copy = pltpu.make_async_copy(probe_hbm, out_ref.at[pl.ds(0, rows), :], sems.at[2])
    solve_copy = pltpu.make_async_copy(solve_hbm, out_ref.at[pl.ds(rows, rows), :], sems.at[3])
    w1_copies = [
        pltpu.make_async_copy(w1_hbm.at[:, pl.ds(j * block, block)], w1_ref.at[:, pl.ds(j * block, block)], sems.at[4 + j])
        for j in range(parts)
    ]
    x_copy.start()
    w1_copies[0].start()
    w2_copy.start()
    for copy in w1_copies[1:]:
        copy.start()
    inv_copy = pltpu.make_async_copy(inv_hbm, inv_ref, sems.at[8])
    inv_copy.start()
    probe_copy.start()
    solve_copy.start()
    x_copy.wait()
    acc = None
    for j in range(parts):
        at = slice(j * block, (j + 1) * block)
        w1_copies[j].wait()
        pre = dot_nn(x_ref[...], w1_ref[:, at])
        hidden = (pre * jax.nn.sigmoid(pre)).astype(BF16)
        if j == 0:
            w2_copy.wait()
        part = dot_nt(hidden, w2t_ref[:, at])
        acc = part if acc is None else acc + part
    inv_copy.wait()
    scaled = (acc * inv_ref[...]).astype(BF16)
    out_ref[2 * rows :, :] = jnp.concatenate([scaled[: rows // 2], scaled[rows // 2 :]], axis=1)
    probe_copy.wait()
    solve_copy.wait()


def encode(inputs, w_first, w2t, inv_row, probes, solves):
    rows = inputs.shape[0]
    return pl.pallas_call(
        encode_body,
        in_specs=[HBM] * 6,
        out_specs=VMEM,
        out_shape=jax.ShapeDtypeStruct((2 * rows + rows // 2, probes.shape[1]), BF16),
        scratch_shapes=[
            pltpu.VMEM(inputs.shape, BF16),
            pltpu.VMEM(w_first.shape, BF16),
            pltpu.VMEM(w2t.shape, BF16),
            pltpu.VMEM(inv_row.shape, F32),
            pltpu.SemaphoreType.DMA((9,)),
        ],
        compiler_params=params(VMEM_MOST),
        name="encode",
    )(inputs, w_first, w2t, inv_row, probes, solves)


def block_parts(ref, own_rows):
    feat = ref.shape[1] // 2
    size = 2 * own_rows + own_rows // 2
    blocks = []
    for at in range(0, ref.shape[0], size):
        packed = ref[at + 2 * own_rows : at + size, :]
        u = jnp.concatenate([packed[:, :feat], packed[:, feat:]], axis=0)
        blocks.append((ref[at : at + own_rows, :], ref[at + own_rows : at + 2 * own_rows, :], u))
    return blocks


def gate_body(sizes, *refs):
    outs = refs[-len(sizes) :]
    at = 0
    for size, out_ref in zip(sizes, outs):
        start = 0
        for ref in refs[at : at + size]:
            out_ref[start : start + ref.shape[0], :] = ref[...]
            start += ref.shape[0]
        at += size


def gate(groups, after=()):
    sizes = [len(group) for group in groups]
    blocks = [block for group in groups for block in group]
    shapes = [jax.ShapeDtypeStruct((sum(b.shape[0] for b in group), group[0].shape[1]), BF16) for group in groups]
    return pl.pallas_call(
        lambda *refs: gate_body(sizes, *refs),
        in_specs=[VMEM] * len(blocks) + [ANY] * len(after),
        out_specs=(VMEM,) * len(groups),
        out_shape=tuple(shapes),
        compiler_params=params(),
        name="gate",
    )(*blocks, *after)


def rows_body(own_rows, count, *refs):
    row_refs, (rowa_ref, rsp_ref) = refs[:count], refs[-2:]
    blocks = [block for ref in row_refs for block in block_parts(ref, own_rows)]
    for b, (p, s, u) in enumerate(blocks):
        at = slice(b * own_rows, (b + 1) * own_rows)
        u32 = u.astype(F32)
        h = -0.5 * jnp.sum(u32 * u32, axis=1, keepdims=True)
        h1 = h.astype(BF16).astype(F32)
        h2 = (h - h1).astype(BF16).astype(F32)
        h3 = h - h1 - h2
        lane = lax.broadcasted_iota(jnp.int32, u.shape, 1)
        tail = jnp.where(lane == 0, h1, jnp.where(lane == 1, h2, jnp.where(lane == 2, h3, 0.0)))
        minus = jnp.full((own_rows, 2 * u.shape[1]), -0.5, BF16)
        rowa_ref[at, :] = jnp.concatenate([u, minus, tail.astype(BF16)], axis=1)
        rsp_ref[at, :] = jnp.concatenate([s, p], axis=1)


def group_rows(own_rows, row_blocks):
    count = len(row_blocks)
    shape = jax.ShapeDtypeStruct((lax.axis_size("kc") * own_rows, 2 * row_blocks[0].shape[1]), BF16)
    return pl.pallas_call(
        lambda *refs: rows_body(own_rows, count, *refs),
        in_specs=[VMEM] * count,
        out_specs=(VMEM, VMEM),
        out_shape=(shape, shape),
        compiler_params=params(),
        name="rows",
    )(*row_blocks)


def pair_body(own_rows, counts, first, last, rowa_ref, rsp_ref, *refs):
    col_refs, refs = refs[: len(counts)], refs[len(counts) :]
    if not first:
        v_in, m_in, s_in = refs[:3]
    if last:
        v_ref, gone_ref, term_ref = refs[-3:]
    else:
        v_ref, m_ref, s_ref = refs[-3:]
    probe = v_ref.shape[1]
    feat = probe // 2
    rows = rowa_ref.shape[0]
    blocks = [block for ref, n in zip(col_refs, counts) for block in block_parts(ref, own_rows)[:n]]
    group = 2
    v, m, sums = (None, None, None) if first else (v_in[...], m_in[...], s_in[...])
    for b in range(0, len(blocks), group):
        pieces = blocks[b : b + group]
        p = jnp.concatenate([q[0] for q in pieces], axis=0)
        s = jnp.concatenate([q[1] for q in pieces], axis=0)
        u = jnp.concatenate([q[2] for q in pieces], axis=0)
        u32 = u.astype(F32)
        sq = u32 * u32
        hi = sq.astype(BF16)
        lo = (sq - hi.astype(F32)).astype(BF16)
        lane = lax.broadcasted_iota(jnp.int32, u.shape, 1)
        ones = jnp.where(lane < 3, 1.0, 0.0).astype(BF16)
        kern = jnp.exp(dot_nt(rowa_ref[...], jnp.concatenate([u, hi, lo, ones], axis=1)))
        one = kern * dot_nt(rsp_ref[:, :probe], p)
        two = kern * dot_nt(rsp_ref[:, probe:], s)
        both = one + two
        lanes = both[:, :128]
        for at in range(128, both.shape[1], 128):
            lanes = lanes + both[:, at : at + 128]
        v_part = dot_nn(kern.astype(BF16), p)
        m_part = dot_nn(one.astype(BF16), u) + dot_nn(two.astype(BF16), u)
        v = v_part if v is None else v + v_part
        m = m_part if m is None else m + m_part
        sums = lanes if sums is None else sums + lanes
    if last:
        v = [v[b * own_rows : (b + 1) * own_rows] for b in range(rows // own_rows)]
        v_ref[...] = jnp.concatenate([v[0], v[1]], axis=0)
        gone_ref[...] = jnp.concatenate([v[2], v[3]], axis=0)
        t = jnp.sum(sums, axis=1, keepdims=True) * rowa_ref[:, :feat].astype(F32) - m
        t = [t[b * own_rows : (b + 1) * own_rows] for b in range(rows // own_rows)]
        term_ref[:own_rows, :] = jnp.concatenate([t[0], t[1]], axis=1)
        term_ref[own_rows:, :] = jnp.concatenate([t[2], t[3]], axis=1)
    else:
        v_ref[...] = v
        m_ref[...] = m
        s_ref[...] = sums


def pairs(own_rows, rowa, rsp, col_blocks, counts, before, last):
    rows, cols = rowa.shape[0], sum(counts) * own_rows
    probe = col_blocks[0].shape[1]
    feat = probe // 2
    first = before is None
    operands = [rowa, rsp] + list(col_blocks) + list(before or ())
    whole = jax.ShapeDtypeStruct((rows, probe), F32)
    half = jax.ShapeDtypeStruct((rows // 2, probe), F32)
    thin = jax.ShapeDtypeStruct((rows, feat), F32)
    return pl.pallas_call(
        lambda *refs: pair_body(own_rows, counts, first, last, *refs),
        in_specs=[VMEM] * len(operands),
        out_specs=(VMEM,) * 3,
        out_shape=(half, half, half) if last else (whole, thin, jax.ShapeDtypeStruct((rows, 128), F32)),
        compiler_params=params(),
        cost_estimate=pl.CostEstimate(flops=1, bytes_accessed=2 * (rows + cols) * 384, transcendentals=0),
        name="pairs",
    )(*operands)


def selection(mine, width, share, order):
    tall, line = lax.axis_size("kr"), lax.axis_size("kc")
    at_row = lax.broadcasted_iota(jnp.int32, (mine, 1), 0)
    piece = at_row // share
    if order:
        owner_line = jnp.zeros_like(piece)
        for i, (deep_mask, tall_mask) in enumerate(order):
            target = (lax.axis_index("enc") ^ deep_mask) * tall + (lax.axis_index("kr") ^ tall_mask)
            owner_line = jnp.where(piece == i, target, owner_line)
        piece = owner_line
    owner = share * (line * piece + lax.axis_index("kc")) + at_row % share
    at_col = lax.broadcasted_iota(jnp.int32, (mine, width), 1)
    return jnp.where(at_col == owner, 1.0, 0.0).astype(BF16)


def prepare_body(share, order, xa_ref, xb_ref, w1_ref, *refs):
    slope_ref, xt_ref, ht_ref = refs[-3:]
    width, hid = w1_ref.shape
    sel = selection(xt_ref.shape[0], width, share, order)
    block = 256
    x = jnp.concatenate([xa_ref[...], xb_ref[...]], axis=0)
    xt_ref[...] = dot_nt(sel, x).astype(BF16)
    ht = None
    for j in range(hid // block):
        at = slice(j * block, (j + 1) * block)
        pre = dot_nn(x, w1_ref[:, at])
        sig = jax.nn.sigmoid(pre)
        hidden = (pre * sig).astype(BF16)
        slope_ref[:, at] = sig * (1.0 + pre * (1.0 - sig))
        part = dot_nt(sel[:, at], hidden)
        ht = part if ht is None else ht + part
    ht_ref[...] = ht.astype(BF16)


def prepare(xa, xb, w_first, share, order, after):
    rows = 2 * xa.shape[0]
    width, hid = w_first.shape
    thin = jax.ShapeDtypeStruct((width // lax.axis_size("kc"), rows), BF16)
    return pl.pallas_call(
        lambda *refs: prepare_body(share, order, *refs),
        in_specs=[VMEM] * 3 + [ANY] * len(after),
        out_specs=(VMEM,) * 3,
        out_shape=(jax.ShapeDtypeStruct((rows, hid), F32), thin, thin),
        compiler_params=params(),
        cost_estimate=pl.CostEstimate(flops=1, bytes_accessed=2**20, transcendentals=0),
        name="prepare",
    )(xa, xb, w_first, *after)


def merge_body(term_ref, got_ref, x_ref, sum_ref, out_ref, passed_ref):
    passed_ref[...] = x_ref[...]
    rows = term_ref.shape[0] // 2
    feat = term_ref.shape[1] // 2
    for at, theirs in ((0, rows), (rows, 0)):
        both = term_ref[at : at + rows, :] + got_ref[theirs : theirs + rows, :]
        sum_ref[at : at + rows, :] = both
        out_ref[at : at + rows, :] = jnp.concatenate([both[:, feat:], both[:, :feat]], axis=1).astype(BF16)


def merge(term, got, x):
    shapes = ((got.shape, F32), (got.shape, BF16), (x.shape, BF16))
    return pl.pallas_call(
        merge_body,
        in_specs=[VMEM] * 3,
        out_specs=(VMEM,) * 3,
        out_shape=tuple(jax.ShapeDtypeStruct(*shape) for shape in shapes),
        compiler_params=params(),
        name="merge",
    )(term, got, x)


def grads_body(pieces, share, scale, term_ref, far_ref, inv_ref, w2t_ref, slope_a, xt_a, ht_a, slope_b, xt_b, ht_b, *out_refs):
    feat, hid = w2t_ref.shape
    half = term_ref.shape[0] // 2
    inv = jnp.concatenate([inv_ref[...], inv_ref[...]], axis=1)
    dfeat = (scale * inv * (term_ref[...] + far_ref[...].astype(F32))).astype(BF16)
    d, e = dfeat[:half, :], dfeat[half:, :]
    dfeat_a = jnp.concatenate([d[:, :feat], e[:, :feat]], axis=0)
    dfeat_b = jnp.concatenate([d[:, feat:], e[:, feat:]], axis=0)
    size = dense_rows(share, hid, feat)

    def store(at, part):
        if pieces is None:
            out_refs[0][:, at : at + part.shape[1]] = part
            return
        row = 0
        for count, ref in zip(pieces, out_refs):
            for n in range(count):
                block = part[row : row + share]
                to = n * size + at * share // 128
                if at < hid:
                    for lane in range(0, part.shape[1], 128):
                        ref[to : to + share, :] = block[:, lane : lane + 128]
                        to += share
                else:
                    half = share // 2
                    ref[to : to + half, :] = jnp.concatenate([block[:half], block[half:]], axis=1)
                row += share

    width = 256
    for at in range(0, hid, width):
        cols = slice(at, at + width)
        dpre_a = (dot_nn(dfeat_a, w2t_ref[:, cols]) * slope_a[:, cols]).astype(BF16)
        dpre_b = (dot_nn(dfeat_b, w2t_ref[:, cols]) * slope_b[:, cols]).astype(BF16)
        store(at, (dot_nn(xt_a[...], dpre_a) + dot_nn(xt_b[...], dpre_b)).astype(BF16))
    store(hid, (dot_nn(ht_a[...], dfeat_a) + dot_nn(ht_b[...], dfeat_b)).astype(BF16))


def dense_rows(share, hid, feat):
    return share * (hid + feat) // 128


def grads(scale, term, far, inv_row, w2t, group_a, group_b, pieces, share):
    feat, hid = w2t.shape
    size = dense_rows(share, hid, feat)
    shapes = [(group_a[1].shape[0], hid + feat)] if pieces is None else [(count * size, 128) for count in pieces]
    return pl.pallas_call(
        lambda *refs: grads_body(pieces, share, scale, *refs),
        in_specs=[VMEM] * 10,
        out_specs=(VMEM,) * len(shapes),
        out_shape=tuple(jax.ShapeDtypeStruct(shape, BF16) for shape in shapes),
        compiler_params=params(),
        name="grads",
    )(term, far, inv_row, w2t, *group_a, *group_b)


def relay_body(count, got_ref, *refs):
    got = got_ref[...].astype(F32)
    start = 0
    for own_ref, out_ref in zip(refs[:count], refs[-count:]):
        size = own_ref.shape[0]
        out_ref[...] = (own_ref[...].astype(F32) + got[start : start + size]).astype(out_ref.dtype)
        start += size


def relay(got, own, kinds, after=()):
    return pl.pallas_call(
        lambda *refs: relay_body(len(own), *refs),
        in_specs=[VMEM] * (1 + len(own)) + [ANY] * len(after),
        out_specs=(VMEM,) * len(own),
        out_shape=tuple(jax.ShapeDtypeStruct(x.shape, kind) for x, kind in zip(own, kinds)),
        compiler_params=params(),
        name="relay",
    )(got, *own, *after)


def total_body(dense, *refs):
    parts, (first_ref, second_ref) = refs[:-2], refs[-2:]
    total = parts[0][...].astype(F32)
    for ref in parts[1:]:
        total = total + ref[...].astype(F32)
    share, hid = first_ref.shape
    feat = second_ref.shape[1]
    if not dense:
        first_ref[...] = total[:, :hid]
        second_ref[...] = total[:, hid:]
        return
    row = 0
    for at in range(0, hid, 128):
        first_ref[:, at : at + 128] = total[row : row + share]
        row += share
    second_ref[: share // 2, :] = total[row:, :feat]
    second_ref[share // 2 :, :] = total[row:, feat:]


def total(parts, share, hid, feat, dense):
    return pl.pallas_call(
        lambda *refs: total_body(dense, *refs),
        in_specs=[VMEM] * len(parts),
        out_specs=(VMEM, VMEM),
        out_shape=(jax.ShapeDtypeStruct((share, hid), F32), jax.ShapeDtypeStruct((share, feat), F32)),
        compiler_params=params(),
        name="total",
    )(*parts)


def hold_body(x_ref, *refs):
    refs[-1][...] = x_ref[...]


def hold(x, after):
    return pl.pallas_call(
        hold_body,
        in_specs=[VMEM] + [ANY] * len(after),
        out_specs=VMEM,
        out_shape=jax.ShapeDtypeStruct(x.shape, x.dtype),
        compiler_params=params(),
        name="hold",
    )(x, *after)


def local(inputs, w_first, w_second, inv_length, probes, solves):
    own_rows, width = inputs.shape
    hid, feat = w_second.shape
    probe_width = probes.shape[1]
    line, deep, tall = lax.axis_size("kc"), lax.axis_size("enc"), lax.axis_size("kr")
    lines = deep * tall
    share = width // (line * lines)
    order = [(2, 1), (3, 1), (1, 1), (0, 1), (2, 0), (3, 0), (1, 0), (0, 0)] if (deep, tall) == (4, 2) else None
    inv_row = inv_length[None, :]
    w2t = w_second.T

    own = encode(inputs, w_first, w2t, inv_row, probes, solves)
    x_core = swap(inputs, "kc", 1)
    group_a = prepare(inputs, x_core, w_first, share, order, (own,))
    far_row = swap(own, "kc", 2)
    tall_masks = range(1, tall)
    if order:
        z_one, z_two, y_own = swap(own, "enc", 1), swap(own, "enc", 2), swap(own, "kr", 1)
        (z_both,) = gate(([z_one, z_two],), (y_own, far_row, group_a[1]))
        (row_both,) = gate(([own, far_row],), (z_both,))
        core_both = swap(row_both, "kc", 1)
        calls = [
            ([row_both, y_own], [1, 1]),
            ([z_one, z_two], [1, 1]),
            ([swap(z_both, "kr", 1)], [2]),
            ([swap(z_two, "enc", 1), swap(y_own, "enc", 3)], [1, 1]),
        ]
    else:
        columns = [own]
        mask = deep // 2
        while mask:
            columns = columns + [swap(block, "enc", mask) for block in columns]
            mask //= 2
        calls = [([block] + [swap(block, "kr", m) for m in tall_masks], [1] * tall) for block in columns]
        (row_both,) = gate(([own, far_row],))
        core_both = swap(row_both, "kc", 1)
    rowa, rsp = group_rows(own_rows, [row_both, core_both])
    x_far = swap(inputs, "kc", 2)

    sofar = None
    for i, (blocks, counts) in enumerate(calls):
        sofar = pairs(own_rows, rowa, rsp, blocks, counts, sofar, i == len(calls) - 1)
    stay, gone, term = sofar
    term, moved, x_sent = merge(term, swap(term, "kc", 1), x_far)
    x_both = swap(x_sent, "kc", 1)
    group_b = prepare(x_far, x_both, w_first, share, order, (term,))
    lscale = loss_gain / math.sqrt(probe_width)
    stay = stay + swap(hold(gone, (term,)), "kc", 1)
    pieces = (2, 1, 1, 1, 1, 1, 1) if order else None
    parts = grads(-lscale, term, swap(moved, "kc", 2), inv_row, w2t, group_a, group_b, pieces, share)
    far = swap(hold(stay[own_rows:], (parts[0],)), "kc", 2)
    if order:
        two, three = relay(swap(parts[0], "kr", 1), parts[3:5], (BF16, BF16))
        (one,) = relay(swap(parts[1], "kr", 1), parts[5:6], (BF16,), (three, far))
        got = [swap(three, "enc", 3), swap(two, "enc", 2), parts[6], swap(one, "enc", 1), swap(parts[2], "kr", 1)]
    else:
        flat = lax.all_to_all(parts[0], ("enc", "kr"), 0, 0, tiled=True)
        got = list(flat.astype(F32).reshape(lines, share, hid + feat))
    grad_first, grad_second = total(got, share, hid, feat, order is not None)

    v = stay[:own_rows] + far
    products = (v * probe_gain).astype(BF16)
    return products, grad_first, grad_second


def solution(mesh):
    rows = P(("enc", "kr", "kc"), None)
    return jax.shard_map(
        local,
        mesh=mesh,
        in_specs=(rows, P(), P(), P(), rows, rows),
        out_specs=(rows, rows, rows),
        check_vma=False,
    )
```

```python
import math

import jax
import jax.numpy as jnp
from jax import lax
from jax.experimental import pallas as pl
from jax.experimental.pallas import tpu as pltpu
from jax.sharding import PartitionSpec as P

probe_gain = 0.5
loss_gain = 0.02
F32 = jnp.float32
BF16 = jnp.bfloat16
VMEM_LIMIT = 48 * 1024 * 1024
VMEM_MOST = 58 * 1024 * 1024
VMEM = pl.BlockSpec(memory_space=pltpu.VMEM)
HBM = pl.BlockSpec(memory_space=pltpu.HBM)
ANY = pl.BlockSpec(memory_space=pl.ANY)


def dot_nn(left, right):
    return lax.dot_general(left, right, (((1,), (0,)), ((), ())), preferred_element_type=F32)


def dot_nt(left, right):
    return lax.dot_general(left, right, (((1,), (1,)), ((), ())), preferred_element_type=F32)


def swap(x, axis, mask):
    size = lax.axis_size(axis)
    return lax.ppermute(x, axis, [(i, i ^ mask) for i in range(size)])


def swap_both(x, deep_mask, tall_mask):
    deep, tall = lax.axis_size("enc"), lax.axis_size("kr")
    pairs_of = [(i, ((i // tall) ^ deep_mask) * tall + ((i % tall) ^ tall_mask)) for i in range(deep * tall)]
    return lax.ppermute(x, ("enc", "kr"), pairs_of)


def swap_split(x, near, far):
    deep, tall, line = lax.axis_size("enc"), lax.axis_size("kr"), lax.axis_size("kc")
    pairs_of = []
    for i in range(deep * tall * line):
        masks = far if i % 2 else near
        pairs_of.append((i, ((i // line // tall) ^ masks[0]) * tall * line + ((i // line % tall) ^ masks[1]) * line + i % line))
    return lax.ppermute(x, ("enc", "kr", "kc"), pairs_of)


def params(limit=VMEM_LIMIT):
    return pltpu.CompilerParams(vmem_limit_bytes=limit)


def encode_body(x_hbm, w1_hbm, w2t_hbm, inv_hbm, probe_hbm, solve_hbm, out_ref, x_ref, w1_ref, w2t_ref, inv_ref, sems):
    rows, width = x_ref.shape
    hid = w1_ref.shape[1]
    parts = 2
    block = hid // parts
    x_copy = pltpu.make_async_copy(x_hbm, x_ref, sems.at[0])
    w2_copy = pltpu.make_async_copy(w2t_hbm, w2t_ref, sems.at[1])
    probe_copy = pltpu.make_async_copy(probe_hbm, out_ref.at[pl.ds(0, rows), :], sems.at[2])
    solve_copy = pltpu.make_async_copy(solve_hbm, out_ref.at[pl.ds(rows, rows), :], sems.at[3])
    w1_copies = [
        pltpu.make_async_copy(w1_hbm.at[:, pl.ds(j * block, block)], w1_ref.at[:, pl.ds(j * block, block)], sems.at[4 + j])
        for j in range(parts)
    ]
    x_copy.start()
    w1_copies[0].start()
    w2_copy.start()
    for copy in w1_copies[1:]:
        copy.start()
    inv_copy = pltpu.make_async_copy(inv_hbm, inv_ref, sems.at[8])
    inv_copy.start()
    probe_copy.start()
    solve_copy.start()
    x_copy.wait()
    acc = None
    for j in range(parts):
        at = slice(j * block, (j + 1) * block)
        w1_copies[j].wait()
        pre = dot_nn(x_ref[...], w1_ref[:, at])
        hidden = (pre * jax.nn.sigmoid(pre)).astype(BF16)
        if j == 0:
            w2_copy.wait()
        part = dot_nt(hidden, w2t_ref[:, at])
        acc = part if acc is None else acc + part
    inv_copy.wait()
    scaled = (acc * inv_ref[...]).astype(BF16)
    out_ref[2 * rows :, :] = jnp.concatenate([scaled[: rows // 2], scaled[rows // 2 :]], axis=1)
    probe_copy.wait()
    solve_copy.wait()


def encode(inputs, w_first, w2t, inv_row, probes, solves):
    rows = inputs.shape[0]
    return pl.pallas_call(
        encode_body,
        in_specs=[HBM] * 6,
        out_specs=VMEM,
        out_shape=jax.ShapeDtypeStruct((2 * rows + rows // 2, probes.shape[1]), BF16),
        scratch_shapes=[
            pltpu.VMEM(inputs.shape, BF16),
            pltpu.VMEM(w_first.shape, BF16),
            pltpu.VMEM(w2t.shape, BF16),
            pltpu.VMEM(inv_row.shape, F32),
            pltpu.SemaphoreType.DMA((9,)),
        ],
        compiler_params=params(VMEM_MOST),
        name="encode",
    )(inputs, w_first, w2t, inv_row, probes, solves)


def block_parts(ref, own_rows):
    feat = ref.shape[1] // 2
    size = 2 * own_rows + own_rows // 2
    blocks = []
    for at in range(0, ref.shape[0], size):
        packed = ref[at + 2 * own_rows : at + size, :]
        u = jnp.concatenate([packed[:, :feat], packed[:, feat:]], axis=0)
        blocks.append((ref[at : at + own_rows, :], ref[at + own_rows : at + 2 * own_rows, :], u))
    return blocks


def gate_body(sizes, *refs):
    outs = refs[-len(sizes) :]
    at = 0
    for size, out_ref in zip(sizes, outs):
        start = 0
        for ref in refs[at : at + size]:
            out_ref[start : start + ref.shape[0], :] = ref[...]
            start += ref.shape[0]
        at += size


def gate(groups, after=()):
    sizes = [len(group) for group in groups]
    blocks = [block for group in groups for block in group]
    shapes = [jax.ShapeDtypeStruct((sum(b.shape[0] for b in group), group[0].shape[1]), BF16) for group in groups]
    return pl.pallas_call(
        lambda *refs: gate_body(sizes, *refs),
        in_specs=[VMEM] * len(blocks) + [ANY] * len(after),
        out_specs=(VMEM,) * len(groups),
        out_shape=tuple(shapes),
        compiler_params=params(),
        name="gate",
    )(*blocks, *after)


def route_body(choices, *refs):
    outs = refs[-len(choices) :]
    odd = lax.rem(lax.axis_index("kc"), 2)
    for side in (0, 1):

        @pl.when(odd == side)
        def _():
            for choice, out_ref in zip(choices, outs):
                out_ref[...] = refs[choice[side]][...]


def route(blocks, choices, after):
    return pl.pallas_call(
        lambda *refs: route_body(choices, *refs),
        in_specs=[VMEM] * len(blocks) + [ANY] * len(after),
        out_specs=(VMEM,) * len(choices),
        out_shape=(jax.ShapeDtypeStruct(blocks[0].shape, BF16),) * len(choices),
        compiler_params=params(),
        name="gate",
    )(*blocks, *after)


def rows_body(own_rows, count, *refs):
    row_refs, (rowa_ref, rsp_ref) = refs[:count], refs[-2:]
    blocks = [block for ref in row_refs for block in block_parts(ref, own_rows)]
    for b, (p, s, u) in enumerate(blocks):
        at = slice(b * own_rows, (b + 1) * own_rows)
        u32 = u.astype(F32)
        h = -0.5 * jnp.sum(u32 * u32, axis=1, keepdims=True)
        h1 = h.astype(BF16).astype(F32)
        h2 = (h - h1).astype(BF16).astype(F32)
        h3 = h - h1 - h2
        lane = lax.broadcasted_iota(jnp.int32, u.shape, 1)
        tail = jnp.where(lane == 0, h1, jnp.where(lane == 1, h2, jnp.where(lane == 2, h3, 0.0)))
        minus = jnp.full((own_rows, 2 * u.shape[1]), -0.5, BF16)
        rowa_ref[at, :] = jnp.concatenate([u, minus, tail.astype(BF16)], axis=1)
        rsp_ref[at, :] = jnp.concatenate([s, p], axis=1)


def group_rows(own_rows, row_blocks):
    count = len(row_blocks)
    shape = jax.ShapeDtypeStruct((lax.axis_size("kc") * own_rows, 2 * row_blocks[0].shape[1]), BF16)
    return pl.pallas_call(
        lambda *refs: rows_body(own_rows, count, *refs),
        in_specs=[VMEM] * count,
        out_specs=(VMEM, VMEM),
        out_shape=(shape, shape),
        compiler_params=params(),
        name="rows",
    )(*row_blocks)


def pair_body(own_rows, counts, first, last, rowa_ref, rsp_ref, *refs):
    col_refs, refs = refs[: len(counts)], refs[len(counts) :]
    if not first:
        v_in, m_in, s_in = refs[:3]
    if last:
        v_ref, gone_ref, term_ref = refs[-3:]
    else:
        v_ref, m_ref, s_ref = refs[-3:]
    probe = v_ref.shape[1]
    feat = probe // 2
    rows = rowa_ref.shape[0]
    blocks = [block for ref, n in zip(col_refs, counts) for block in block_parts(ref, own_rows)[:n]]
    p_all, s_all, u_all = (jnp.concatenate([block[i] for block in blocks], axis=0) for i in range(3))
    cols = len(blocks) * own_rows
    tile = 256 if cols % 256 == 0 else 2 * own_rows
    v, m, sums = (None, None, None) if first else (v_in[...], m_in[...], s_in[...])
    for b in range(0, cols, tile):
        p, s, u = p_all[b : b + tile], s_all[b : b + tile], u_all[b : b + tile]
        u32 = u.astype(F32)
        sq = u32 * u32
        hi = sq.astype(BF16)
        lo = (sq - hi.astype(F32)).astype(BF16)
        lane = lax.broadcasted_iota(jnp.int32, u.shape, 1)
        ones = jnp.where(lane < 3, 1.0, 0.0).astype(BF16)
        kern = jnp.exp(dot_nt(rowa_ref[...], jnp.concatenate([u, hi, lo, ones], axis=1)))
        one = kern * dot_nt(rsp_ref[:, :probe], p)
        two = kern * dot_nt(rsp_ref[:, probe:], s)
        both = one + two
        lanes = both[:, :128]
        for at in range(128, both.shape[1], 128):
            lanes = lanes + both[:, at : at + 128]
        v_part = dot_nn(kern.astype(BF16), p)
        m_part = dot_nn(one.astype(BF16), u) + dot_nn(two.astype(BF16), u)
        v = v_part if v is None else v + v_part
        m = m_part if m is None else m + m_part
        sums = lanes if sums is None else sums + lanes
    if last:
        v = [v[b * own_rows : (b + 1) * own_rows] for b in range(rows // own_rows)]
        v_ref[...] = jnp.concatenate([v[0], v[1]], axis=0)
        gone_ref[...] = jnp.concatenate([v[2], v[3]], axis=0)
        t = jnp.sum(sums, axis=1, keepdims=True) * rowa_ref[:, :feat].astype(F32) - m
        t = [t[b * own_rows : (b + 1) * own_rows] for b in range(rows // own_rows)]
        term_ref[:own_rows, :] = jnp.concatenate([t[0], t[1]], axis=1)
        term_ref[own_rows:, :] = jnp.concatenate([t[2], t[3]], axis=1)
    else:
        v_ref[...] = v
        m_ref[...] = m
        s_ref[...] = sums


def pairs(own_rows, rowa, rsp, col_blocks, counts, before, last):
    rows, cols = rowa.shape[0], sum(counts) * own_rows
    probe = col_blocks[0].shape[1]
    feat = probe // 2
    first = before is None
    operands = [rowa, rsp] + list(col_blocks) + list(before or ())
    whole = jax.ShapeDtypeStruct((rows, probe), F32)
    half = jax.ShapeDtypeStruct((rows // 2, probe), F32)
    thin = jax.ShapeDtypeStruct((rows, feat), F32)
    return pl.pallas_call(
        lambda *refs: pair_body(own_rows, counts, first, last, *refs),
        in_specs=[VMEM] * len(operands),
        out_specs=(VMEM,) * 3,
        out_shape=(half, half, half) if last else (whole, thin, jax.ShapeDtypeStruct((rows, 128), F32)),
        compiler_params=params(),
        cost_estimate=pl.CostEstimate(flops=1, bytes_accessed=2 * (rows + cols) * 384, transcendentals=0),
        name="pairs",
    )(*operands)


def selection(mine, width, share, order):
    tall, line = lax.axis_size("kr"), lax.axis_size("kc")
    at_row = lax.broadcasted_iota(jnp.int32, (mine, 1), 0)
    piece = at_row // share
    if order:
        owner_line = jnp.zeros_like(piece)
        for i, (deep_mask, tall_mask) in enumerate(order):
            target = (lax.axis_index("enc") ^ deep_mask) * tall + (lax.axis_index("kr") ^ tall_mask)
            owner_line = jnp.where(piece == i, target, owner_line)
        piece = owner_line
    owner = share * (line * piece + lax.axis_index("kc")) + at_row % share
    at_col = lax.broadcasted_iota(jnp.int32, (mine, width), 1)
    return jnp.where(at_col == owner, 1.0, 0.0).astype(BF16)


def prepare_body(share, order, xa_ref, xb_ref, w1_ref, *refs):
    slope_ref, xt_ref, ht_ref = refs[-3:]
    width, hid = w1_ref.shape
    sel = selection(xt_ref.shape[0], width, share, order)
    block = 256
    x = jnp.concatenate([xa_ref[...], xb_ref[...]], axis=0)
    xt_ref[...] = dot_nt(sel, x).astype(BF16)
    ht = None
    for j in range(hid // block):
        at = slice(j * block, (j + 1) * block)
        pre = dot_nn(x, w1_ref[:, at])
        sig = jax.nn.sigmoid(pre)
        hidden = (pre * sig).astype(BF16)
        slope_ref[:, at] = sig * (1.0 + pre * (1.0 - sig))
        part = dot_nt(sel[:, at], hidden)
        ht = part if ht is None else ht + part
    ht_ref[...] = ht.astype(BF16)


def prepare(xa, xb, w_first, share, order, after):
    rows = 2 * xa.shape[0]
    width, hid = w_first.shape
    thin = jax.ShapeDtypeStruct((width // lax.axis_size("kc"), rows), BF16)
    return pl.pallas_call(
        lambda *refs: prepare_body(share, order, *refs),
        in_specs=[VMEM] * 3 + [ANY] * len(after),
        out_specs=(VMEM,) * 3,
        out_shape=(jax.ShapeDtypeStruct((rows, hid), F32), thin, thin),
        compiler_params=params(),
        cost_estimate=pl.CostEstimate(flops=1, bytes_accessed=2**20, transcendentals=0),
        name="prepare",
    )(xa, xb, w_first, *after)


def merge_body(term_ref, got_ref, x_ref, sum_ref, out_ref, passed_ref):
    passed_ref[...] = x_ref[...]
    rows = term_ref.shape[0] // 2
    feat = term_ref.shape[1] // 2
    for at, theirs in ((0, rows), (rows, 0)):
        both = term_ref[at : at + rows, :] + got_ref[theirs : theirs + rows, :]
        sum_ref[at : at + rows, :] = both
        out_ref[at : at + rows, :] = jnp.concatenate([both[:, feat:], both[:, :feat]], axis=1).astype(BF16)


def merge(term, got, x):
    shapes = ((got.shape, F32), (got.shape, BF16), (x.shape, BF16))
    return pl.pallas_call(
        merge_body,
        in_specs=[VMEM] * 3,
        out_specs=(VMEM,) * 3,
        out_shape=tuple(jax.ShapeDtypeStruct(*shape) for shape in shapes),
        compiler_params=params(),
        name="merge",
    )(term, got, x)


def grads_body(pieces, share, scale, term_ref, far_ref, inv_ref, w2t_ref, slope_a, xt_a, ht_a, slope_b, xt_b, ht_b, *out_refs):
    feat, hid = w2t_ref.shape
    half = term_ref.shape[0] // 2
    inv = jnp.concatenate([inv_ref[...], inv_ref[...]], axis=1)
    dfeat = (scale * inv * (term_ref[...] + far_ref[...].astype(F32))).astype(BF16)
    d, e = dfeat[:half, :], dfeat[half:, :]
    dfeat_a = jnp.concatenate([d[:, :feat], e[:, :feat]], axis=0)
    dfeat_b = jnp.concatenate([d[:, feat:], e[:, feat:]], axis=0)
    size = dense_rows(share, hid, feat)

    def store(at, part):
        if pieces is None:
            out_refs[0][:, at : at + part.shape[1]] = part
            return
        row = 0
        for count, ref in zip(pieces, out_refs):
            for n in range(count):
                block = part[row : row + share]
                to = n * size + at * share // 128
                if at < hid:
                    for lane in range(0, part.shape[1], 128):
                        ref[to : to + share, :] = block[:, lane : lane + 128]
                        to += share
                else:
                    half = share // 2
                    ref[to : to + half, :] = jnp.concatenate([block[:half], block[half:]], axis=1)
                row += share

    width = 256
    for at in range(0, hid, width):
        cols = slice(at, at + width)
        dpre_a = (dot_nn(dfeat_a, w2t_ref[:, cols]) * slope_a[:, cols]).astype(BF16)
        dpre_b = (dot_nn(dfeat_b, w2t_ref[:, cols]) * slope_b[:, cols]).astype(BF16)
        store(at, (dot_nn(xt_a[...], dpre_a) + dot_nn(xt_b[...], dpre_b)).astype(BF16))
    store(hid, (dot_nn(ht_a[...], dfeat_a) + dot_nn(ht_b[...], dfeat_b)).astype(BF16))


def dense_rows(share, hid, feat):
    return share * (hid + feat) // 128


def grads(scale, term, far, inv_row, w2t, group_a, group_b, pieces, share):
    feat, hid = w2t.shape
    size = dense_rows(share, hid, feat)
    shapes = [(group_a[1].shape[0], hid + feat)] if pieces is None else [(count * size, 128) for count in pieces]
    return pl.pallas_call(
        lambda *refs: grads_body(pieces, share, scale, *refs),
        in_specs=[VMEM] * 10,
        out_specs=(VMEM,) * len(shapes),
        out_shape=tuple(jax.ShapeDtypeStruct(shape, BF16) for shape in shapes),
        compiler_params=params(),
        name="grads",
    )(term, far, inv_row, w2t, *group_a, *group_b)


def relay_body(count, got_ref, *refs):
    got = got_ref[...].astype(F32)
    start = 0
    for own_ref, out_ref in zip(refs[:count], refs[-count:]):
        size = own_ref.shape[0]
        out_ref[...] = (own_ref[...].astype(F32) + got[start : start + size]).astype(out_ref.dtype)
        start += size


def relay(got, own, kinds, after=()):
    return pl.pallas_call(
        lambda *refs: relay_body(len(own), *refs),
        in_specs=[VMEM] * (1 + len(own)) + [ANY] * len(after),
        out_specs=(VMEM,) * len(own),
        out_shape=tuple(jax.ShapeDtypeStruct(x.shape, kind) for x, kind in zip(own, kinds)),
        compiler_params=params(),
        name="relay",
    )(got, *own, *after)


def total_body(dense, *refs):
    parts, (first_ref, second_ref) = refs[:-2], refs[-2:]
    total = parts[0][...].astype(F32)
    for ref in parts[1:]:
        total = total + ref[...].astype(F32)
    share, hid = first_ref.shape
    feat = second_ref.shape[1]
    if not dense:
        first_ref[...] = total[:, :hid]
        second_ref[...] = total[:, hid:]
        return
    row = 0
    for at in range(0, hid, 128):
        first_ref[:, at : at + 128] = total[row : row + share]
        row += share
    second_ref[: share // 2, :] = total[row:, :feat]
    second_ref[share // 2 :, :] = total[row:, feat:]


def total(parts, share, hid, feat, dense):
    return pl.pallas_call(
        lambda *refs: total_body(dense, *refs),
        in_specs=[VMEM] * len(parts),
        out_specs=(VMEM, VMEM),
        out_shape=(jax.ShapeDtypeStruct((share, hid), F32), jax.ShapeDtypeStruct((share, feat), F32)),
        compiler_params=params(),
        name="total",
    )(*parts)


def hold_body(x_ref, *refs):
    refs[-1][...] = x_ref[...]


def hold(x, after):
    return pl.pallas_call(
        hold_body,
        in_specs=[VMEM] + [ANY] * len(after),
        out_specs=VMEM,
        out_shape=jax.ShapeDtypeStruct(x.shape, x.dtype),
        compiler_params=params(),
        name="hold",
    )(x, *after)


def local(inputs, w_first, w_second, inv_length, probes, solves):
    own_rows, width = inputs.shape
    hid, feat = w_second.shape
    probe_width = probes.shape[1]
    line, deep, tall = lax.axis_size("kc"), lax.axis_size("enc"), lax.axis_size("kr")
    lines = deep * tall
    share = width // (line * lines)
    order = [(2, 1), (3, 1), (1, 1), (0, 1), (2, 0), (3, 0), (1, 0), (0, 0)] if (deep, tall) == (4, 2) else None
    inv_row = inv_length[None, :]
    w2t = w_second.T

    own = encode(inputs, w_first, w2t, inv_row, probes, solves)
    x_core = swap(inputs, "kc", 1)
    group_a = prepare(inputs, x_core, w_first, share, order, (own,))
    far_row = swap(own, "kc", 2)
    tall_masks = range(1, tall)
    if order:
        z_one, z_two, y_own = swap(own, "enc", 1), swap(own, "enc", 2), swap(own, "kr", 1)
        a, b, c, d = route([z_one, z_two, y_own], [(0, 1), (1, 2), (1, 0), (2, 1)], (far_row, group_a[1]))
        (row_both,) = gate(([own, far_row],), (a,))
        core_both = swap(row_both, "kc", 1)
        over = (0, 1)
        calls = [
            ([row_both, y_own, z_one, z_two], [1, 1, 1, 1]),
            ([swap_split(a, over, (1, 0)), swap_split(b, over, (3, 0))], [1, 1]),
            ([swap_split(c, (1, 0), over), swap_split(d, (3, 0), over)], [1, 1]),
        ]
    else:
        columns = [own]
        mask = deep // 2
        while mask:
            columns = columns + [swap(block, "enc", mask) for block in columns]
            mask //= 2
        calls = [([block] + [swap(block, "kr", m) for m in tall_masks], [1] * tall) for block in columns]
        (row_both,) = gate(([own, far_row],))
        core_both = swap(row_both, "kc", 1)
    rowa, rsp = group_rows(own_rows, [row_both, core_both])
    x_far = swap(inputs, "kc", 2)

    sofar = None
    for i, (blocks, counts) in enumerate(calls):
        sofar = pairs(own_rows, rowa, rsp, blocks, counts, sofar, i == len(calls) - 1)
    stay, gone, term = sofar
    term, moved, x_sent = merge(term, swap(term, "kc", 1), x_far)
    x_both = swap(x_sent, "kc", 1)
    group_b = prepare(x_far, x_both, w_first, share, order, (term,))
    lscale = loss_gain / math.sqrt(probe_width)
    stay = stay + swap(hold(gone, (term,)), "kc", 1)
    pieces = (2, 1, 1, 1, 1, 1, 1) if order else None
    parts = grads(-lscale, term, swap(moved, "kc", 2), inv_row, w2t, group_a, group_b, pieces, share)
    far = swap(hold(stay[own_rows:], (parts[0],)), "kc", 2)
    if order:
        two, three = relay(swap(parts[0], "kr", 1), parts[3:5], (BF16, BF16))
        (one,) = relay(swap(parts[1], "kr", 1), parts[5:6], (BF16,), (three, far))
        got = [swap(three, "enc", 3), swap(two, "enc", 2), parts[6], swap(one, "enc", 1), swap(parts[2], "kr", 1)]
    else:
        flat = lax.all_to_all(parts[0], ("enc", "kr"), 0, 0, tiled=True)
        got = list(flat.astype(F32).reshape(lines, share, hid + feat))
    grad_first, grad_second = total(got, share, hid, feat, order is not None)

    v = stay[:own_rows] + far
    products = (v * probe_gain).astype(BF16)
    return products, grad_first, grad_second


def solution(mesh):
    rows = P(("enc", "kr", "kc"), None)
    return jax.shard_map(
        local,
        mesh=mesh,
        in_specs=(rows, P(), P(), P(), rows, rows),
        out_specs=(rows, rows, rows),
        check_vma=False,
    )
```

```python
import math

import jax
import jax.numpy as jnp
from jax import lax
from jax.experimental import pallas as pl
from jax.experimental.pallas import tpu as pltpu
from jax.sharding import PartitionSpec as P

probe_gain = 0.5
loss_gain = 0.02
F32 = jnp.float32
BF16 = jnp.bfloat16
VMEM_LIMIT = 48 * 1024 * 1024
VMEM_MOST = 58 * 1024 * 1024
VMEM = pl.BlockSpec(memory_space=pltpu.VMEM)
HBM = pl.BlockSpec(memory_space=pltpu.HBM)
ANY = pl.BlockSpec(memory_space=pl.ANY)


def dot_nn(left, right):
    return lax.dot_general(left, right, (((1,), (0,)), ((), ())), preferred_element_type=F32)


def dot_nt(left, right):
    return lax.dot_general(left, right, (((1,), (1,)), ((), ())), preferred_element_type=F32)


def swap(x, axis, mask):
    size = lax.axis_size(axis)
    return lax.ppermute(x, axis, [(i, i ^ mask) for i in range(size)])


def swap_both(x, deep_mask, tall_mask):
    deep, tall = lax.axis_size("enc"), lax.axis_size("kr")
    pairs_of = [(i, ((i // tall) ^ deep_mask) * tall + ((i % tall) ^ tall_mask)) for i in range(deep * tall)]
    return lax.ppermute(x, ("enc", "kr"), pairs_of)


def swap_split(x, near, far):
    deep, tall, line = lax.axis_size("enc"), lax.axis_size("kr"), lax.axis_size("kc")
    pairs_of = []
    for i in range(deep * tall * line):
        masks = far if i % 2 else near
        pairs_of.append((i, ((i // line // tall) ^ masks[0]) * tall * line + ((i // line % tall) ^ masks[1]) * line + i % line))
    return lax.ppermute(x, ("enc", "kr", "kc"), pairs_of)


def params(limit=VMEM_LIMIT):
    return pltpu.CompilerParams(vmem_limit_bytes=limit)


def encode_body(x_hbm, w1_hbm, w2t_hbm, inv_hbm, probe_hbm, solve_hbm, out_ref, x_ref, w1_ref, w2t_ref, inv_ref, sems):
    rows, width = x_ref.shape
    hid = w1_ref.shape[1]
    parts = 2
    block = hid // parts
    x_copy = pltpu.make_async_copy(x_hbm, x_ref, sems.at[0])
    w2_copy = pltpu.make_async_copy(w2t_hbm, w2t_ref, sems.at[1])
    probe_copy = pltpu.make_async_copy(probe_hbm, out_ref.at[pl.ds(0, rows), :], sems.at[2])
    solve_copy = pltpu.make_async_copy(solve_hbm, out_ref.at[pl.ds(rows, rows), :], sems.at[3])
    deep = width // 2
    w1_copies = [
        [
            pltpu.make_async_copy(
                w1_hbm.at[pl.ds(n * deep, deep), pl.ds(j * block, block)],
                w1_ref.at[pl.ds(n * deep, deep), pl.ds(j * block, block)],
                sems.at[4 + 2 * j + n],
            )
            for n in range(2)
        ]
        for j in range(parts)
    ]
    x_copy.start()
    for copy in w1_copies[0]:
        copy.start()
    w2_copy.start()
    for copies in w1_copies[1:]:
        for copy in copies:
            copy.start()
    inv_copy = pltpu.make_async_copy(inv_hbm, inv_ref, sems.at[8])
    inv_copy.start()
    probe_copy.start()
    solve_copy.start()
    x_copy.wait()
    acc = None
    for j in range(parts):
        at = slice(j * block, (j + 1) * block)
        for copy in w1_copies[j]:
            copy.wait()
        pre = dot_nn(x_ref[...], w1_ref[:, at])
        hidden = (pre * jax.nn.sigmoid(pre)).astype(BF16)
        if j == 0:
            w2_copy.wait()
        part = dot_nt(hidden, w2t_ref[:, at])
        acc = part if acc is None else acc + part
    inv_copy.wait()
    scaled = (acc * inv_ref[...]).astype(BF16)
    out_ref[2 * rows :, :] = jnp.concatenate([scaled[: rows // 2], scaled[rows // 2 :]], axis=1)
    probe_copy.wait()
    solve_copy.wait()


def encode(inputs, w_first, w2t, inv_row, probes, solves):
    rows = inputs.shape[0]
    return pl.pallas_call(
        encode_body,
        in_specs=[HBM] * 6,
        out_specs=VMEM,
        out_shape=jax.ShapeDtypeStruct((2 * rows + rows // 2, probes.shape[1]), BF16),
        scratch_shapes=[
            pltpu.VMEM(inputs.shape, BF16),
            pltpu.VMEM(w_first.shape, BF16),
            pltpu.VMEM(w2t.shape, BF16),
            pltpu.VMEM(inv_row.shape, F32),
            pltpu.SemaphoreType.DMA((9,)),
        ],
        compiler_params=params(VMEM_MOST),
        name="encode",
    )(inputs, w_first, w2t, inv_row, probes, solves)


def block_parts(ref, own_rows):
    feat = ref.shape[1] // 2
    size = 2 * own_rows + own_rows // 2
    blocks = []
    for at in range(0, ref.shape[0], size):
        packed = ref[at + 2 * own_rows : at + size, :]
        u = jnp.concatenate([packed[:, :feat], packed[:, feat:]], axis=0)
        blocks.append((ref[at : at + own_rows, :], ref[at + own_rows : at + 2 * own_rows, :], u))
    return blocks


def gate_body(sizes, *refs):
    outs = refs[-len(sizes) :]
    at = 0
    for size, out_ref in zip(sizes, outs):
        start = 0
        for ref in refs[at : at + size]:
            out_ref[start : start + ref.shape[0], :] = ref[...]
            start += ref.shape[0]
        at += size


def gate(groups, after=()):
    sizes = [len(group) for group in groups]
    blocks = [block for group in groups for block in group]
    shapes = [jax.ShapeDtypeStruct((sum(b.shape[0] for b in group), group[0].shape[1]), BF16) for group in groups]
    return pl.pallas_call(
        lambda *refs: gate_body(sizes, *refs),
        in_specs=[VMEM] * len(blocks) + [ANY] * len(after),
        out_specs=(VMEM,) * len(groups),
        out_shape=tuple(shapes),
        compiler_params=params(),
        name="gate",
    )(*blocks, *after)


def route_body(choices, *refs):
    outs = refs[-len(choices) :]
    odd = lax.rem(lax.axis_index("kc"), 2)
    for side in (0, 1):

        @pl.when(odd == side)
        def _():
            for choice, out_ref in zip(choices, outs):
                out_ref[...] = refs[choice[side]][...]


def route(blocks, choices, after):
    return pl.pallas_call(
        lambda *refs: route_body(choices, *refs),
        in_specs=[VMEM] * len(blocks) + [ANY] * len(after),
        out_specs=(VMEM,) * len(choices),
        out_shape=(jax.ShapeDtypeStruct(blocks[0].shape, BF16),) * len(choices),
        compiler_params=params(),
        name="gate",
    )(*blocks, *after)


def rows_body(own_rows, count, *refs):
    row_refs, (rowa_ref, rsp_ref) = refs[:count], refs[-2:]
    blocks = [block for ref in row_refs for block in block_parts(ref, own_rows)]
    for b, (p, s, u) in enumerate(blocks):
        at = slice(b * own_rows, (b + 1) * own_rows)
        u32 = u.astype(F32)
        h = -0.5 * jnp.sum(u32 * u32, axis=1, keepdims=True)
        h1 = h.astype(BF16).astype(F32)
        h2 = (h - h1).astype(BF16).astype(F32)
        h3 = h - h1 - h2
        lane = lax.broadcasted_iota(jnp.int32, u.shape, 1)
        tail = jnp.where(lane == 0, h1, jnp.where(lane == 1, h2, jnp.where(lane == 2, h3, 0.0)))
        minus = jnp.full((own_rows, 2 * u.shape[1]), -0.5, BF16)
        rowa_ref[at, :] = jnp.concatenate([u, minus, tail.astype(BF16)], axis=1)
        rsp_ref[at, :] = jnp.concatenate([s, p], axis=1)


def group_rows(own_rows, row_blocks):
    count = len(row_blocks)
    shape = jax.ShapeDtypeStruct((lax.axis_size("kc") * own_rows, 2 * row_blocks[0].shape[1]), BF16)
    return pl.pallas_call(
        lambda *refs: rows_body(own_rows, count, *refs),
        in_specs=[VMEM] * count,
        out_specs=(VMEM, VMEM),
        out_shape=(shape, shape),
        compiler_params=params(),
        name="rows",
    )(*row_blocks)


def pair_body(own_rows, counts, first, last, rowa_ref, rsp_ref, *refs):
    col_refs, refs = refs[: len(counts)], refs[len(counts) :]
    if not first:
        v_in, m_in, s_in = refs[:3]
    if last:
        v_ref, gone_ref, term_ref = refs[-3:]
    else:
        v_ref, m_ref, s_ref = refs[-3:]
    probe = v_ref.shape[1]
    feat = probe // 2
    rows = rowa_ref.shape[0]
    blocks = [block for ref, n in zip(col_refs, counts) for block in block_parts(ref, own_rows)[:n]]
    group = 2
    v, m, sums = (None, None, None) if first else (v_in[...], m_in[...], s_in[...])
    for b in range(0, len(blocks), group):
        pieces = blocks[b : b + group]
        p = jnp.concatenate([q[0] for q in pieces], axis=0)
        s = jnp.concatenate([q[1] for q in pieces], axis=0)
        u = jnp.concatenate([q[2] for q in pieces], axis=0)
        u32 = u.astype(F32)
        sq = u32 * u32
        hi = sq.astype(BF16)
        lo = (sq - hi.astype(F32)).astype(BF16)
        lane = lax.broadcasted_iota(jnp.int32, u.shape, 1)
        ones = jnp.where(lane < 3, 1.0, 0.0).astype(BF16)
        kern = jnp.exp(dot_nt(rowa_ref[...], jnp.concatenate([u, hi, lo, ones], axis=1)))
        one = kern * dot_nt(rsp_ref[:, :probe], p)
        two = kern * dot_nt(rsp_ref[:, probe:], s)
        both = one + two
        lanes = both[:, :128]
        for at in range(128, both.shape[1], 128):
            lanes = lanes + both[:, at : at + 128]
        v_part = dot_nn(kern.astype(BF16), p)
        m_part = dot_nn(one.astype(BF16), u) + dot_nn(two.astype(BF16), u)
        v = v_part if v is None else v + v_part
        m = m_part if m is None else m + m_part
        sums = lanes if sums is None else sums + lanes
    if last:
        v = [v[b * own_rows : (b + 1) * own_rows] for b in range(rows // own_rows)]
        v_ref[...] = jnp.concatenate([v[0], v[1]], axis=0)
        gone_ref[...] = jnp.concatenate([v[2], v[3]], axis=0)
        t = jnp.sum(sums, axis=1, keepdims=True) * rowa_ref[:, :feat].astype(F32) - m
        t = [t[b * own_rows : (b + 1) * own_rows] for b in range(rows // own_rows)]
        term_ref[:own_rows, :] = jnp.concatenate([t[0], t[1]], axis=1)
        term_ref[own_rows:, :] = jnp.concatenate([t[2], t[3]], axis=1)
    else:
        v_ref[...] = v
        m_ref[...] = m
        s_ref[...] = sums


def pairs(own_rows, rowa, rsp, col_blocks, counts, before, last):
    rows, cols = rowa.shape[0], sum(counts) * own_rows
    probe = col_blocks[0].shape[1]
    feat = probe // 2
    first = before is None
    operands = [rowa, rsp] + list(col_blocks) + list(before or ())
    whole = jax.ShapeDtypeStruct((rows, probe), F32)
    half = jax.ShapeDtypeStruct((rows // 2, probe), F32)
    thin = jax.ShapeDtypeStruct((rows, feat), F32)
    return pl.pallas_call(
        lambda *refs: pair_body(own_rows, counts, first, last, *refs),
        in_specs=[VMEM] * len(operands),
        out_specs=(VMEM,) * 3,
        out_shape=(half, half, half) if last else (whole, thin, jax.ShapeDtypeStruct((rows, 128), F32)),
        compiler_params=params(),
        cost_estimate=pl.CostEstimate(flops=1, bytes_accessed=2 * (rows + cols) * 384, transcendentals=0),
        name="pairs",
    )(*operands)


def selection(mine, width, share, order):
    tall, line = lax.axis_size("kr"), lax.axis_size("kc")
    at_row = lax.broadcasted_iota(jnp.int32, (mine, 1), 0)
    piece = at_row // share
    if order:
        owner_line = jnp.zeros_like(piece)
        for i, (deep_mask, tall_mask) in enumerate(order):
            target = (lax.axis_index("enc") ^ deep_mask) * tall + (lax.axis_index("kr") ^ tall_mask)
            owner_line = jnp.where(piece == i, target, owner_line)
        piece = owner_line
    owner = share * (line * piece + lax.axis_index("kc")) + at_row % share
    at_col = lax.broadcasted_iota(jnp.int32, (mine, width), 1)
    return jnp.where(at_col == owner, 1.0, 0.0).astype(BF16)


def prepare_body(share, order, xa_ref, xb_ref, w1_ref, *refs):
    slope_ref, xt_ref, ht_ref = refs[-3:]
    width, hid = w1_ref.shape
    sel = selection(xt_ref.shape[0], width, share, order)
    block = 256
    x = jnp.concatenate([xa_ref[...], xb_ref[...]], axis=0)
    xt_ref[...] = dot_nt(sel, x).astype(BF16)
    ht = None
    for j in range(hid // block):
        at = slice(j * block, (j + 1) * block)
        pre = dot_nn(x, w1_ref[:, at])
        sig = jax.nn.sigmoid(pre)
        hidden = (pre * sig).astype(BF16)
        slope_ref[:, at] = sig * (1.0 + pre * (1.0 - sig))
        part = dot_nt(sel[:, at], hidden)
        ht = part if ht is None else ht + part
    ht_ref[...] = ht.astype(BF16)


def prepare(xa, xb, w_first, share, order, after):
    rows = 2 * xa.shape[0]
    width, hid = w_first.shape
    thin = jax.ShapeDtypeStruct((width // lax.axis_size("kc"), rows), BF16)
    return pl.pallas_call(
        lambda *refs: prepare_body(share, order, *refs),
        in_specs=[VMEM] * 3 + [ANY] * len(after),
        out_specs=(VMEM,) * 3,
        out_shape=(jax.ShapeDtypeStruct((rows, hid), F32), thin, thin),
        compiler_params=params(),
        cost_estimate=pl.CostEstimate(flops=1, bytes_accessed=2**20, transcendentals=0),
        name="prepare",
    )(xa, xb, w_first, *after)


def merge_body(term_ref, got_ref, x_ref, sum_ref, out_ref, passed_ref):
    passed_ref[...] = x_ref[...]
    rows = term_ref.shape[0] // 2
    feat = term_ref.shape[1] // 2
    for at, theirs in ((0, rows), (rows, 0)):
        both = term_ref[at : at + rows, :] + got_ref[theirs : theirs + rows, :]
        sum_ref[at : at + rows, :] = both
        out_ref[at : at + rows, :] = jnp.concatenate([both[:, feat:], both[:, :feat]], axis=1).astype(BF16)


def merge(term, got, x):
    shapes = ((got.shape, F32), (got.shape, BF16), (x.shape, BF16))
    return pl.pallas_call(
        merge_body,
        in_specs=[VMEM] * 3,
        out_specs=(VMEM,) * 3,
        out_shape=tuple(jax.ShapeDtypeStruct(*shape) for shape in shapes),
        compiler_params=params(),
        name="merge",
    )(term, got, x)


def grads_body(pieces, share, scale, term_ref, far_ref, inv_ref, w2t_ref, slope_a, xt_a, ht_a, slope_b, xt_b, ht_b, *out_refs):
    feat, hid = w2t_ref.shape
    half = term_ref.shape[0] // 2
    inv = jnp.concatenate([inv_ref[...], inv_ref[...]], axis=1)
    dfeat = (scale * inv * (term_ref[...] + far_ref[...].astype(F32))).astype(BF16)
    d, e = dfeat[:half, :], dfeat[half:, :]
    dfeat_a = jnp.concatenate([d[:, :feat], e[:, :feat]], axis=0)
    dfeat_b = jnp.concatenate([d[:, feat:], e[:, feat:]], axis=0)
    size = dense_rows(share, hid, feat)

    def store(at, part):
        if pieces is None:
            out_refs[0][:, at : at + part.shape[1]] = part
            return
        row = 0
        for count, ref in zip(pieces, out_refs):
            for n in range(count):
                block = part[row : row + share]
                to = n * size + at * share // 128
                if at < hid:
                    for lane in range(0, part.shape[1], 128):
                        ref[to : to + share, :] = block[:, lane : lane + 128]
                        to += share
                else:
                    half = share // 2
                    ref[to : to + half, :] = jnp.concatenate([block[:half], block[half:]], axis=1)
                row += share

    width = 256
    for at in range(0, hid, width):
        cols = slice(at, at + width)
        dpre_a = (dot_nn(dfeat_a, w2t_ref[:, cols]) * slope_a[:, cols]).astype(BF16)
        dpre_b = (dot_nn(dfeat_b, w2t_ref[:, cols]) * slope_b[:, cols]).astype(BF16)
        store(at, (dot_nn(xt_a[...], dpre_a) + dot_nn(xt_b[...], dpre_b)).astype(BF16))
    store(hid, (dot_nn(ht_a[...], dfeat_a) + dot_nn(ht_b[...], dfeat_b)).astype(BF16))


def dense_rows(share, hid, feat):
    return share * (hid + feat) // 128


def grads(scale, term, far, inv_row, w2t, group_a, group_b, pieces, share):
    feat, hid = w2t.shape
    size = dense_rows(share, hid, feat)
    shapes = [(group_a[1].shape[0], hid + feat)] if pieces is None else [(count * size, 128) for count in pieces]
    return pl.pallas_call(
        lambda *refs: grads_body(pieces, share, scale, *refs),
        in_specs=[VMEM] * 10,
        out_specs=(VMEM,) * len(shapes),
        out_shape=tuple(jax.ShapeDtypeStruct(shape, BF16) for shape in shapes),
        compiler_params=params(),
        name="grads",
    )(term, far, inv_row, w2t, *group_a, *group_b)


def relay_body(count, got_ref, *refs):
    got = got_ref[...].astype(F32)
    start = 0
    for own_ref, out_ref in zip(refs[:count], refs[-count:]):
        size = own_ref.shape[0]
        out_ref[...] = (own_ref[...].astype(F32) + got[start : start + size]).astype(out_ref.dtype)
        start += size


def relay(got, own, kinds, after=()):
    return pl.pallas_call(
        lambda *refs: relay_body(len(own), *refs),
        in_specs=[VMEM] * (1 + len(own)) + [ANY] * len(after),
        out_specs=(VMEM,) * len(own),
        out_shape=tuple(jax.ShapeDtypeStruct(x.shape, kind) for x, kind in zip(own, kinds)),
        compiler_params=params(),
        name="relay",
    )(got, *own, *after)


def total_body(dense, *refs):
    parts, (first_ref, second_ref) = refs[:-2], refs[-2:]
    total = parts[0][...].astype(F32)
    for ref in parts[1:]:
        total = total + ref[...].astype(F32)
    share, hid = first_ref.shape
    feat = second_ref.shape[1]
    if not dense:
        first_ref[...] = total[:, :hid]
        second_ref[...] = total[:, hid:]
        return
    row = 0
    for at in range(0, hid, 128):
        first_ref[:, at : at + 128] = total[row : row + share]
        row += share
    second_ref[: share // 2, :] = total[row:, :feat]
    second_ref[share // 2 :, :] = total[row:, feat:]


def total(parts, share, hid, feat, dense):
    return pl.pallas_call(
        lambda *refs: total_body(dense, *refs),
        in_specs=[VMEM] * len(parts),
        out_specs=(VMEM, VMEM),
        out_shape=(jax.ShapeDtypeStruct((share, hid), F32), jax.ShapeDtypeStruct((share, feat), F32)),
        compiler_params=params(),
        name="total",
    )(*parts)


def hold_body(x_ref, *refs):
    refs[-1][...] = x_ref[...]


def hold(x, after):
    return pl.pallas_call(
        hold_body,
        in_specs=[VMEM] + [ANY] * len(after),
        out_specs=VMEM,
        out_shape=jax.ShapeDtypeStruct(x.shape, x.dtype),
        compiler_params=params(),
        name="hold",
    )(x, *after)


def local(inputs, w_first, w_second, inv_length, probes, solves):
    own_rows, width = inputs.shape
    hid, feat = w_second.shape
    probe_width = probes.shape[1]
    line, deep, tall = lax.axis_size("kc"), lax.axis_size("enc"), lax.axis_size("kr")
    lines = deep * tall
    share = width // (line * lines)
    order = [(2, 1), (3, 1), (1, 1), (0, 1), (2, 0), (3, 0), (1, 0), (0, 0)] if (deep, tall) == (4, 2) else None
    inv_row = inv_length[None, :]
    w2t = w_second.T

    own = encode(inputs, w_first, w2t, inv_row, probes, solves)
    x_core = swap(inputs, "kc", 1)
    group_a = prepare(inputs, x_core, w_first, share, order, (own,))
    far_row = swap(own, "kc", 2)
    tall_masks = range(1, tall)
    if order:
        z_one, z_two, y_own = swap(own, "enc", 1), swap(own, "enc", 2), swap(own, "kr", 1)
        a, b, c, d = route([z_one, z_two, y_own], [(0, 1), (1, 2), (1, 0), (2, 1)], (far_row, group_a[1]))
        (row_both,) = gate(([own, far_row],), (a,))
        core_both = swap(row_both, "kc", 1)
        over = (0, 1)
        calls = [
            ([row_both, y_own], [1, 1]),
            ([z_one, z_two], [1, 1]),
            ([swap_split(a, over, (1, 0)), swap_split(b, over, (3, 0))], [1, 1]),
            ([swap_split(c, (1, 0), over), swap_split(d, (3, 0), over)], [1, 1]),
        ]
    else:
        columns = [own]
        mask = deep // 2
        while mask:
            columns = columns + [swap(block, "enc", mask) for block in columns]
            mask //= 2
        calls = [([block] + [swap(block, "kr", m) for m in tall_masks], [1] * tall) for block in columns]
        (row_both,) = gate(([own, far_row],))
        core_both = swap(row_both, "kc", 1)
    rowa, rsp = group_rows(own_rows, [row_both, core_both])
    x_far = swap(inputs, "kc", 2)

    sofar = None
    for i, (blocks, counts) in enumerate(calls):
        sofar = pairs(own_rows, rowa, rsp, blocks, counts, sofar, i == len(calls) - 1)
    stay, gone, term = sofar
    term, moved, x_sent = merge(term, swap(term, "kc", 1), x_far)
    x_both = swap(x_sent, "kc", 1)
    group_b = prepare(x_far, x_both, w_first, share, order, (term,))
    lscale = loss_gain / math.sqrt(probe_width)
    stay = stay + swap(hold(gone, (term,)), "kc", 1)
    pieces = (2, 1, 1, 1, 1, 1, 1) if order else None
    parts = grads(-lscale, term, swap(moved, "kc", 2), inv_row, w2t, group_a, group_b, pieces, share)
    far = swap(hold(stay[own_rows:], (parts[0],)), "kc", 2)
    if order:
        two, three = relay(swap(parts[0], "kr", 1), parts[3:5], (BF16, BF16))
        (one,) = relay(swap(parts[1], "kr", 1), parts[5:6], (BF16,), (three, far))
        got = [swap(three, "enc", 3), swap(two, "enc", 2), parts[6], swap(one, "enc", 1), swap(parts[2], "kr", 1)]
    else:
        flat = lax.all_to_all(parts[0], ("enc", "kr"), 0, 0, tiled=True)
        got = list(flat.astype(F32).reshape(lines, share, hid + feat))
    grad_first, grad_second = total(got, share, hid, feat, order is not None)

    v = stay[:own_rows] + far
    products = (v * probe_gain).astype(BF16)
    return products, grad_first, grad_second


def solution(mesh):
    rows = P(("enc", "kr", "kc"), None)
    return jax.shard_map(
        local,
        mesh=mesh,
        in_specs=(rows, P(), P(), P(), rows, rows),
        out_specs=(rows, rows, rows),
        check_vma=False,
    )
```
